32 devices in a mesh: tgt: 4 (over y, x), hist: 8 (over z, core).
Axes of the slice: x: 2, y: 2, z: 4, core: 2. Of those that a mesh axis runs over, the one named last changes fastest.
Arguments:
- history: float32 [2, 32, 32, 128, 128], P(None, 'hist', 'tgt'), may hold values from -6 to 6
- self_energy: float32 [2, 32, 128, 128], P(None, 'hist'), may hold values from -6 to 6
- green_row: float32 [2, 32, 128, 128], P(None, 'tgt'), may hold values from -6 to 6
- propagator: float32 [2, 128, 128], replicated, may hold values from -0.375 to 0.375
Outputs:
- new_rows: float32 [4, 2, 32, 128, 128], P(None, None, 'tgt', 'hist')
The draws below stay inside these ranges and needn't reach their ends.
All inputs are finite; a program needn't handle non-finite values.
Results may differ from the reference program's by a relative error of at most 0.00016.
Values sent between devices are 32-bit elements; how exact they have to be, the bound alone decides.
A program may use at most 64 MiB of HBM per device.

```python
import jax
import jax.numpy as jnp
from jax import lax

N = 128
SH = 4
STEPS = 4
TW = 32
TT = 8


def block_levels(stream_key, shape, shards, smallest, top_value):
    loudness, own = 1.0, jax.random.fold_in(stream_key, 6)
    for axis_at, parts in shards:
        steps = jnp.exp(jax.random.uniform(jax.random.fold_in(own, axis_at), (parts,), jnp.float32, smallest / len(shards), top_value / len(shards)))
        loudness = loudness * jnp.repeat(steps, shape[axis_at] // parts).reshape([-1 if axis == axis_at else 1 for axis in range(len(shape))])
    return loudness


def noise(rng, shape, spread, most, split=(), held_as=jnp.bfloat16):
    values = jax.random.normal(rng, shape, jnp.float32) * spread
    if len(split) > 0:
        values = block_levels(rng, shape, split, -0.22, 0.18) * values
    return jnp.clip(values, min=-most, max=most).astype(held_as)


def setup_inputs(seed: int = 0) -> dict:
    arg_keys = jax.random.split(jax.random.key(seed), 5)
    return {
        "history": noise(arg_keys[0], (2, TW, TW, N, N), 1.0, 6.0, ((1, 8), (2, 4)), jnp.float32),
        "self_energy": noise(arg_keys[1], (2, TW, N, N), 1.0, 6.0, ((1, 8),), jnp.float32),
        "green_row": noise(arg_keys[2], (2, TW, N, N), 1.0, 6.0, ((1, 4),), jnp.float32),
        "propagator": noise(arg_keys[3], (2, N, N), (2 * N) ** -0.5, 0.375, (), jnp.float32),
    }


COUPLING = 1.5
MIXING = 0.7


def complex_product(left, right, form):
    highest = lax.Precision.HIGHEST
    real_part = jnp.einsum(form, left[0], right[0], precision=highest) - jnp.einsum(form, left[1], right[1], precision=highest)
    imag_part = jnp.einsum(form, left[0], right[1], precision=highest) + jnp.einsum(form, left[1], right[0], precision=highest)
    return real_part, imag_part


def self_energy_of(green):
    modulus = green[0] * green[0] + green[1] * green[1]
    factor = -COUPLING * modulus / (1.0 + modulus)
    return jnp.stack([factor * green[0], factor * green[1]])


def collide(self_energy, history):
    norm_factor = float(TW * N) ** -0.5

    def block_terms(index):
        section = lax.dynamic_slice_in_dim(history, index * TT, TT, 2)
        real_part, imag_part = complex_product(self_energy, section, "sik,stkj->tij")
        return jnp.stack([real_part, imag_part]) * norm_factor

    blocks = lax.map(block_terms, jnp.arange(TW // TT, dtype=jnp.int32))
    return jnp.moveaxis(blocks, 0, 1).reshape(2, TW, N, N)


def reference(history, self_energy, green_row, propagator):
    new_rows = []
    for step_index in range(STEPS):
        collision = collide(self_energy, history)
        prop_real, prop_imag = complex_product(propagator, green_row, "ik,tkj->tij")
        green_row = jnp.stack([MIXING * (prop_real + collision[1]), MIXING * (prop_imag - collision[0])])
        new_rows.append(green_row)
        self_energy = self_energy_of(green_row)
        history = lax.dynamic_update_slice_in_dim(history, green_row[:, None], step_index * SH, 1)
    return jnp.stack(new_rows)
```

```python
import functools

import jax
import jax.numpy as jnp
from jax import lax
from jax.experimental import pallas as pl
from jax.experimental.pallas import tpu as pltpu
from jax.sharding import PartitionSpec as P

STEPS = 4
COUPLING = 1.5
MIXING = 0.7
MESH = pl.DeviceIdType.MESH
F32, BF16 = jnp.float32, jnp.bfloat16


def split(value):
    high = value.astype(BF16)
    return high, (value - high.astype(F32)).astype(BF16)


def complex_of(product):
    n = product.shape[0] // 2
    return product[:n, :n] - product[n:, n:], product[:n, n:] + product[n:, :n]


def snake(index):
    q, r = index // 2, index % 2
    return 2 * q + r + (q % 2) * (1 - 2 * r)


def kernel(
    n_tgt, n_hist, norm,
    h_hbm, s_hbm, r_hbm, p_hbm, out_ref,
    hst, h3, s3, sbuf, rin, pin, exs, exr, own, upb, dnb, rows, x3, base, sxb, l3, outb,
    fin, exf, fsum, upf, dnf,
    h_sem, in_sem, ex_s, ex_r, ch_s, up_r, dn_r, rg_s, rg_r, sx_s, sx_r, bd_s, bd_r,
    fx_s, fx_r, fc_s, fu_r, fd_r,
):
    _, sh, tt_all, n, _ = h_hbm.shape
    hp = n_hist // n_tgt
    nz = n_hist // hp
    band = n // n_hist
    depth = sh * n
    g, h = lax.axis_index("tgt"), lax.axis_index("hist")
    z, c = h // hp, h % hp
    root = z == g
    pos = snake(g)
    rel = (pos - snake(z) + n_tgt) % n_tgt
    ahead, behind = snake((pos + 1) % n_tgt), snake((pos + n_tgt - 1) % n_tgt)
    last = STEPS - 1
    sends = []

    def remote(src, dst, send_sem, recv_sem, tgt, hist):
        return pltpu.make_async_remote_copy(
            src_ref=src, dst_ref=dst, send_sem=send_sem, recv_sem=recv_sem,
            device_id={"tgt": tgt, "hist": hist}, device_id_type=MESH,
        )

    def loop(count, body):
        lax.fori_loop(0, count, lambda i, _: (body(i), None)[1], None)

    def h_copy(t):
        return pltpu.make_async_copy(h_hbm.at[:, :, t], hst.at[t], h_sem.at[t])

    s_copy = pltpu.make_async_copy(s_hbm, sbuf.at[0], in_sem.at[0])
    p_copy = pltpu.make_async_copy(p_hbm, pin, in_sem.at[1])
    r_copy = pltpu.make_async_copy(r_hbm, rin, in_sem.at[2])
    s_copy.start()
    for d in [*range(1, hp), 0]:
        loop(sh, lambda t, d=d: h_copy((c + d) % hp * sh + t).start())
    p_copy.start()
    r_copy.start()

    barrier = pltpu.get_barrier_semaphore()
    for e in range(1, n_hist):
        pl.semaphore_signal(
            barrier, inc=1, device_id={"tgt": g, "hist": (h + e) % n_hist}, device_id_type=MESH
        )
    for near in (ahead, behind):
        pl.semaphore_signal(barrier, inc=1, device_id={"tgt": near, "hist": h}, device_id_type=MESH)

    def store_x3(slot, tt, real, imag):
        for at, value in ((0, real), (n, imag)):
            high, low = split(value)
            cols = pl.ds(at, n)
            x3[slot, tt, pl.ds(0, n), cols] = high
            x3[slot, tt, pl.ds(n, n), cols] = low
            x3[slot, tt, pl.ds(2 * n, n), cols] = high

    def store_l3(slot, real, imag):
        for at, value in ((0, real), (n, imag)):
            high, low = split(value)
            l3[slot, pl.ds(at, n), pl.ds(0, n)] = high
            l3[slot, pl.ds(at, n), pl.ds(n, n)] = high
            l3[slot, pl.ds(at, n), pl.ds(2 * n, n)] = low

    def store_s3(step):
        for s in range(sh):
            for part in range(2):
                high, low = split(sbuf[step, part, s])
                r = pl.ds(part * n, n)
                s3[r, pl.ds(s * n, n)] = high
                s3[r, pl.ds(depth + s * n, n)] = high
                s3[r, pl.ds(2 * depth + s * n, n)] = low
        if step > 0:

            @pl.when(h < step)
            def _():
                for at in range(3):
                    s3[:, pl.ds(at * depth, n)] = jnp.zeros((2 * n, n), BF16)

    def store_h3(t):
        h_copy(t).wait()
        for s in range(sh):
            for part in range(2):
                high, low = split(hst[t, part, s])
                cols = pl.ds(part * n, n)
                h3[t, pl.ds(s * n, n), cols] = high
                h3[t, pl.ds(depth + s * n, n), cols] = low
                h3[t, pl.ds(2 * depth + s * n, n), cols] = high

    def term(t, step):
        if step == 0:
            store_h3(t)
        real, imag = complex_of(jnp.dot(s3[...], h3[t], preferred_element_type=F32))
        return (MIXING * norm) * imag, (-MIXING * norm) * real

    def ex_copy(step, d, tt):
        return remote(
            exs.at[step, d, tt], exr.at[step, d, tt], ex_s.at[step, d, tt], ex_r.at[step, d, tt],
            g, z * hp + (c + d) % hp,
        )

    def chain_copy(step, tt, up):
        return remote(
            own.at[step, tt], (upb if up else dnb).at[step, tt], ch_s.at[step, tt],
            (up_r if up else dn_r).at[step, tt], g, h + hp if up else h - hp,
        )

    def ring_copy(step, part, s):
        ref = sbuf.at[step, part, s]
        return remote(
            ref, ref, rg_s.at[step, part, s], rg_r.at[step, part, s],
            behind if part else ahead, h,
        )

    ring_gets = (rel > 0, rel > 0)
    ring_gives = (rel < n_tgt - 1, rel != 1)

    def sx_copy(step, k, to):
        return remote(
            sbuf.at[step, :, 0], sxb.at[step, k], sx_s.at[step, k, to], sx_r.at[step, k],
            g, g * hp + to,
        )

    def band_copy(step, e, sender):
        to = (h + e) % n_hist
        return remote(
            rows.at[step, :, :, pl.ds(pl.multiple_of(to * band, band), band)],
            outb.at[step, :, pl.ds(sender * sh, sh)], bd_s.at[step, e], bd_r.at[step, sender],
            g, to,
        )

    def fin_ex_copy(q, d):
        to = (c + d) % hp
        return remote(
            fin.at[q, :, to], exf.at[q, d], fx_s.at[q, d], fx_r.at[q, d], g, z * hp + to
        )

    def fin_chain_copy(q, zz, up):
        return remote(
            fsum.at[q, zz], (upf if up else dnf).at[q, zz], fc_s.at[q, zz],
            (fu_r if up else fd_r).at[q, zz], g, h + hp if up else h - hp,
        )

    def receive_s(step):
        def one(s):
            for part in range(2):

                @pl.when(ring_gets[part])
                def _():
                    ring_copy(step, part, s).wait_recv()

                    @pl.when(ring_gives[part])
                    def _():
                        ring_copy(step, part, s).start()

        loop(sh, one)
        for part in range(2):
            sends.append(
                (ring_gives[part], lambda part=part: loop(sh, lambda s: ring_copy(step, part, s).wait_send()))
            )
        for k in range(min(step, n_hist)):
            for to in range(hp):
                mine = g * hp + to == h

                @pl.when((h == k) & mine)
                def _():
                    sxb[step, k] = sbuf[step, :, 0]

                away = (h == k) & (g * hp + to != h)

                @pl.when(away)
                def _():
                    sx_copy(step, k, to).start()

                sends.append((away, lambda k=k, to=to: sx_copy(step, k, to).wait_send()))

    def make_base(step):
        for k in range(min(step, n_hist)):

            @pl.when(h != k)
            def _():
                sx_copy(step, k, 0).wait_recv()

            store_l3(k + 1, norm * sxb[step, k, 1], -norm * sxb[step, k, 0])

        def one(tt):
            total = jnp.dot(l3[0], x3[step, tt], preferred_element_type=F32)
            for k in range(min(step, n_hist)):
                total += jnp.dot(l3[k + 1], x3[k + 1, tt], preferred_element_type=F32)
            real, imag = complex_of(total)
            base[tt, 0] = MIXING * real
            base[tt, 1] = MIXING * imag

        loop(sh, one)

    s_copy.wait()
    store_s3(0)
    pl.semaphore_wait(barrier, n_hist + 1)

    for step in range(last):
        if step > 0:
            receive_s(step)
            store_s3(step)

        for d in range(1, hp):

            def give(tt, d=d):
                real, imag = term((c + d) % hp * sh + tt, step)
                exs[step, d, tt, 0] = real
                exs[step, d, tt, 1] = imag
                ex_copy(step, d, tt).start()

            loop(sh, give)
            sends.append((None, lambda d=d, step=step: loop(sh, lambda tt: ex_copy(step, d, tt).wait_send())))

        def keep(tt):
            real, imag = term(c * sh + tt, step)
            own[step, tt, 0] = real
            own[step, tt, 1] = imag
            for d in range(1, hp):
                ex_copy(step, d, tt).wait_recv()
                own[step, tt] += exr[step, d, tt]

            @pl.when((z < g) & (z == 0))
            def _():
                chain_copy(step, tt, True).start()

            @pl.when((z > g) & (z == nz - 1))
            def _():
                chain_copy(step, tt, False).start()

        loop(sh, keep)
        if step == 0:
            p_copy.wait()
            r_copy.wait()

        @pl.when(root)
        def _():
            if step == 0:
                store_l3(0, pin[0], pin[1])
                loop(sh, lambda tt: store_x3(0, tt, rin[0, c * sh + tt], rin[1, c * sh + tt]))
            make_base(step)

        def link(tt):
            @pl.when((z > 0) & (z <= g))
            def _():
                chain_copy(step, tt, True).wait_recv()
                own[step, tt] += upb[step, tt]

            @pl.when((z < nz - 1) & (z >= g))
            def _():
                chain_copy(step, tt, False).wait_recv()
                own[step, tt] += dnb[step, tt]

            @pl.when((z < g) & (z > 0))
            def _():
                chain_copy(step, tt, True).start()

            @pl.when((z > g) & (z < nz - 1))
            def _():
                chain_copy(step, tt, False).start()

            @pl.when(root)
            def _():
                real = own[step, tt, 0] + base[tt, 0]
                imag = own[step, tt, 1] + base[tt, 1]
                modulus = real * real + imag * imag
                factor = -COUPLING * modulus / (1.0 + modulus)
                sbuf[step + 1, 0, tt] = factor * real
                sbuf[step + 1, 1, tt] = factor * imag
                ring_copy(step + 1, 0, tt).start()
                ring_copy(step + 1, 1, tt).start()
                rows[step, 0, tt] = real
                rows[step, 1, tt] = imag
                store_x3(step + 1, tt, real, imag)

        loop(sh, link)
        for up, gives in ((True, z < g), (False, z > g)):
            sends.append(
                (gives, lambda up=up, step=step: loop(sh, lambda tt: chain_copy(step, tt, up).wait_send()))
            )

        @pl.when(root)
        def _():
            outb[step, :, pl.ds(c * sh, sh)] = rows[
                step, :, :, pl.ds(pl.multiple_of(h * band, band), band)
            ]
            loop(n_hist - 1, lambda e: band_copy(step, e + 1, c).start())

        sends.append(
            (root, lambda step=step: loop(n_hist - 1, lambda e: band_copy(step, e + 1, c).wait_send()))
        )

    receive_s(last)
    store_s3(last)
    pl.when(root)(lambda: make_base(last))
    for q in range(hp):

        def bands(tt, q=q):
            for part, value in enumerate(term(q * sh + tt, last)):
                for b in range(n_hist):
                    fin[q, b // hp, b % hp, tt, part] = value[b * band : (b + 1) * band]

        loop(sh, bands)

        @pl.when(root & (c == q))
        def _():
            def add(tt):
                for part in range(2):
                    for b in range(n_hist):
                        fin[q, b // hp, b % hp, tt, part] += base[tt, part, pl.ds(b * band, band)]

            loop(sh, add)

        for d in range(1, hp):
            fin_ex_copy(q, d).start()
            sends.append((None, lambda q=q, d=d: fin_ex_copy(q, d).wait_send()))

    for q in range(hp):
        for d in range(1, hp):
            fin_ex_copy(q, d).wait_recv()

        def both(zz, q=q):
            value = fin[q, zz, c]
            for d in range(1, hp):
                value += exf[q, d, zz]
            fsum[q, zz] = value

        loop(nz, both)
        for dist in range(nz - 1, 0, -1):
            for up in (True, False):
                zz = z + dist if up else z - dist
                on_way = zz < nz if up else zz >= 0
                first = z == 0 if up else z == nz - 1

                @pl.when(on_way)
                def _():
                    @pl.when(jnp.logical_not(first))
                    def _():
                        fin_chain_copy(q, zz, up).wait_recv()
                        fsum[q, zz] += (upf if up else dnf)[q, zz]

                    fin_chain_copy(q, zz, up).start()

                sends.append(
                    (on_way, lambda q=q, zz=zz, up=up: fin_chain_copy(q, zz, up).wait_send())
                )
    for q in range(hp):

        @pl.when(z > 0)
        def _():
            fin_chain_copy(q, z, True).wait_recv()
            fsum[q, z] += upf[q, z]

        @pl.when(z < nz - 1)
        def _():
            fin_chain_copy(q, z, False).wait_recv()
            fsum[q, z] += dnf[q, z]

        for tt in range(sh):
            for part in range(2):
                out_ref[last, part, q * sh + tt] = fsum[q, z, tt, part]

    for step in range(last):
        for sender in range(hp):

            @pl.when(h != g * hp + sender)
            def _():
                band_copy(step, 1, sender).wait_recv()

        out_ref[step] = outb[step]

    for gives, wait in sends:
        if gives is None:
            wait()
        else:
            pl.when(gives)(wait)


def per_device(history, self_energy, green_row, propagator):
    n_tgt, n_hist = lax.axis_size("tgt"), lax.axis_size("hist")
    _, sh, tt, n, _ = history.shape
    hp, band, last = n_hist // n_tgt, n // n_hist, STEPS - 1
    nz = n_hist // hp
    norm = float(sh * n_hist * n) ** (-0.5)
    vmem, sem = pltpu.VMEM, pltpu.SemaphoreType.DMA
    return pl.pallas_call(
        functools.partial(kernel, n_tgt, n_hist, norm),
        out_shape=jax.ShapeDtypeStruct((STEPS, 2, tt, band, n), F32),
        in_specs=[pl.BlockSpec(memory_space=pl.ANY)] * 4,
        out_specs=pl.BlockSpec(memory_space=pltpu.VMEM),
        scratch_shapes=[
            vmem((tt, 2, sh, n, n), F32),
            vmem((tt, 3 * sh * n, 2 * n), BF16),
            vmem((2 * n, 3 * sh * n), BF16),
            vmem((STEPS, 2, sh, n, n), F32),
            vmem((2, tt, n, n), F32),
            vmem((2, n, n), F32),
            vmem((last, hp, sh, 2, n, n), F32),
            vmem((last, hp, sh, 2, n, n), F32),
            vmem((last, sh, 2, n, n), F32),
            vmem((last, sh, 2, n, n), F32),
            vmem((last, sh, 2, n, n), F32),
            vmem((last, 2, sh, n, n), F32),
            vmem((STEPS, sh, 3 * n, 2 * n), BF16),
            vmem((sh, 2, n, n), F32),
            vmem((STEPS, STEPS, 2, n, n), F32),
            vmem((STEPS, 2 * n, 3 * n), BF16),
            vmem((last, 2, tt, band, n), F32),
            vmem((hp, nz, hp, sh, 2, band, n), F32),
            vmem((hp, hp, nz, sh, 2, band, n), F32),
            vmem((hp, nz, sh, 2, band, n), F32),
            vmem((hp, nz, sh, 2, band, n), F32),
            vmem((hp, nz, sh, 2, band, n), F32),
            sem((tt,)),
            sem((3,)),
            sem((last, hp, sh)),
            sem((last, hp, sh)),
            sem((last, sh)),
            sem((last, sh)),
            sem((last, sh)),
            sem((STEPS, 2, sh)),
            sem((STEPS, 2, sh)),
            sem((STEPS, STEPS, hp)),
            sem((STEPS, STEPS)),
            sem((last, n_hist)),
            sem((last, hp)),
            sem((hp, hp)),
            sem((hp, hp)),
            sem((hp, nz)),
            sem((hp, nz)),
            sem((hp, nz)),
        ],
        compiler_params=pltpu.CompilerParams(
            collective_id=0, has_side_effects=True, vmem_limit_bytes=56 * 2**20
        ),
    )(history, self_energy, green_row, propagator)


def solution(mesh):
    in_specs = (
        P(None, "hist", "tgt", None, None),
        P(None, "hist", None, None),
        P(None, "tgt", None, None),
        P(),
    )
    out_specs = P(None, None, "tgt", "hist", None)
    return jax.shard_map(
        per_device, mesh=mesh, in_specs=in_specs, out_specs=out_specs, check_vma=False
    )
```

```python
import functools

import jax
import jax.numpy as jnp
from jax import lax
from jax.experimental import pallas as pl
from jax.experimental.pallas import tpu as pltpu
from jax.sharding import PartitionSpec as P

STEPS = 4
COUPLING = 1.5
MIXING = 0.7
MESH = pl.DeviceIdType.MESH
PIECES = 2
F32, BF16 = jnp.float32, jnp.bfloat16


def split(value):
    high = value.astype(BF16)
    return high, (value - high.astype(F32)).astype(BF16)


def complex_of(product):
    n = product.shape[0] // 2
    return product[:n, :n] - product[n:, n:], product[:n, n:] + product[n:, :n]


def snake(index):
    q, r = index // 2, index % 2
    return 2 * q + r + (q % 2) * (1 - 2 * r)


def kernel(
    n_tgt, n_hist, norm,
    h_hbm, s_hbm, r_hbm, p_hbm, out_ref,
    hst, h3, s3, acc, sbuf, rin, pin, exs, exr, own, upb, dnb, rows, x3, base, sxb, l3, outb,
    fin, exf, fsum, upf, dnf,
    h_sem, in_sem, ex_s, ex_r, ch_s, up_r, dn_r, rg_s, rg_r, sx_s, sy_s, sx_r, bd_s, bd_r,
    fx_s, fx_r, fc_s, fu_r, fd_r,
):
    _, sh, tt_all, n, _ = h_hbm.shape
    hp = n_hist // n_tgt
    nz = n_hist // hp
    band = n // n_hist
    depth = sh * n
    g, h = lax.axis_index("tgt"), lax.axis_index("hist")
    z, c = h // hp, h % hp
    root = z == g
    pos = snake(g)
    rel = (pos - snake(z) + n_tgt) % n_tgt
    ahead, behind = snake((pos + 1) % n_tgt), snake((pos + n_tgt - 1) % n_tgt)
    last = STEPS - 1
    sends = []

    def remote(src, dst, send_sem, recv_sem, tgt, hist):
        return pltpu.make_async_remote_copy(
            src_ref=src, dst_ref=dst, send_sem=send_sem, recv_sem=recv_sem,
            device_id={"tgt": tgt, "hist": hist}, device_id_type=MESH,
        )

    def loop(count, body):
        lax.fori_loop(0, count, lambda i, _: (body(i), None)[1], None)

    def h_copy(t):
        return pltpu.make_async_copy(h_hbm.at[:, :, t], hst.at[t], h_sem.at[t])

    s_copy = pltpu.make_async_copy(s_hbm, sbuf.at[0], in_sem.at[0])
    p_copy = pltpu.make_async_copy(p_hbm, pin, in_sem.at[1])
    r_copy = pltpu.make_async_copy(r_hbm, rin, in_sem.at[2])
    s_copy.start()
    for d in [*range(1, hp), 0]:
        loop(sh, lambda t, d=d: h_copy((c + d) % hp * sh + t).start())
    p_copy.start()
    r_copy.start()

    barrier = pltpu.get_barrier_semaphore()
    for e in range(1, n_hist):
        pl.semaphore_signal(
            barrier, inc=1, device_id={"tgt": g, "hist": (h + e) % n_hist}, device_id_type=MESH
        )
    for near in (ahead, behind):
        pl.semaphore_signal(barrier, inc=1, device_id={"tgt": near, "hist": h}, device_id_type=MESH)

    def store_x3(slot, tt, real, imag):
        for at, value in ((0, real), (n, imag)):
            high, low = split(value)
            cols = pl.ds(at, n)
            x3[slot, tt, pl.ds(0, n), cols] = high
            x3[slot, tt, pl.ds(n, n), cols] = low
            x3[slot, tt, pl.ds(2 * n, n), cols] = high

    def store_l3(slot, real, imag):
        for at, value in ((0, real), (n, imag)):
            high, low = split(value)
            l3[slot, pl.ds(at, n), pl.ds(0, n)] = high
            l3[slot, pl.ds(at, n), pl.ds(n, n)] = high
            l3[slot, pl.ds(at, n), pl.ds(2 * n, n)] = low

    width = 3 * n

    def store_s3(step, s):
        for part in range(2):
            high, low = split(sbuf[step, part, s])
            r = pl.ds(part * n, n)
            s3[r, pl.ds(s * width, n)] = high
            s3[r, pl.ds(s * width + n, n)] = high
            s3[r, pl.ds(s * width + 2 * n, n)] = low
        if step > 0 and s == 0:

            @pl.when(h < step)
            def _():
                s3[:, pl.ds(0, width)] = jnp.zeros((2 * n, width), BF16)

    def store_h3(t):
        h_copy(t).wait()
        for s in range(sh):
            for part in range(2):
                high, low = split(hst[t, part, s])
                cols = pl.ds(part * n, n)
                h3[t, pl.ds(s * width, n), cols] = high
                h3[t, pl.ds(s * width + n, n), cols] = low
                h3[t, pl.ds(s * width + 2 * n, n), cols] = high

    def dot_of(t, begin, end):
        at = pl.ds(begin * width, (end - begin) * width)
        return jnp.dot(s3[:, at], h3[t, at, :], preferred_element_type=F32)

    def term(t, step):
        if step == 0:
            store_h3(t)
            product = dot_of(t, 0, sh)
        else:
            product = acc[t] + dot_of(t, sh - 1, sh)
        real, imag = complex_of(product)
        return (MIXING * norm) * imag, (-MIXING * norm) * real

    def ex_copy(step, d, tt):
        return remote(
            exs.at[step, d, tt], exr.at[step, d, tt], ex_s.at[step, d, tt], ex_r.at[step, d, tt],
            g, z * hp + (c + d) % hp,
        )

    def piece(p):
        per_part = PIECES // 2
        return p // per_part, pl.ds(p % per_part * (n // per_part), n // per_part)

    def chain_copy(step, tt, p, up):
        part, at = piece(p)
        return remote(
            own.at[step, tt, part, at], (upb if up else dnb).at[step, tt, part, at],
            ch_s.at[step, tt, p], (up_r if up else dn_r).at[step, tt, p],
            g, h + hp if up else h - hp,
        )

    def ring_copy(step, part, s, way):
        ref = sbuf.at[step, part, s]
        return remote(
            ref, ref, rg_s.at[step, way, part, s], rg_r.at[step, part, s],
            behind if way else ahead, h,
        )

    reach = (n_tgt // 2, n_tgt // 2 - 1)
    ring_gives = [(rel < reach[p], (rel == 0) | (rel >= reach[p] + 2)) for p in range(2)]

    def ring_give(step, s, part, way):
        @pl.when(ring_gives[part][way])
        def _():
            ring_copy(step, part, s, way).start()

    def sx_copy(step, k):
        return remote(
            sbuf.at[step, :, 0], sxb.at[step, k], sx_s.at[step, k], sx_r.at[step, k],
            g, g * hp + k % hp,
        )

    def sy_copy(step, k, d):
        return remote(
            sxb.at[step, k], sxb.at[step, k], sy_s.at[step, k, d], sx_r.at[step, k],
            g, z * hp + (c + d) % hp,
        )

    def band_copy(step, e, sender):
        to = (h + e) % n_hist
        return remote(
            rows.at[step, :, :, pl.ds(pl.multiple_of(to * band, band), band)],
            outb.at[step, :, pl.ds(sender * sh, sh)], bd_s.at[step, e], bd_r.at[step, sender],
            g, to,
        )

    def fin_ex_copy(q, d):
        to = (c + d) % hp
        return remote(
            fin.at[q, :, to], exf.at[q, d], fx_s.at[q, d], fx_r.at[q, d], g, z * hp + to
        )

    def fin_chain_copy(q, zz, up):
        return remote(
            fsum.at[q, zz], (upf if up else dnf).at[q, zz], fc_s.at[q, zz],
            (fu_r if up else fd_r).at[q, zz], g, h + hp if up else h - hp,
        )

    def receive_s(step, s):
        @pl.when(rel > 0)
        def _():
            for part in range(2):
                ring_copy(step, part, s, 0).wait_recv()
                ring_give(step, s, part, 0)
                ring_give(step, s, part, 1)

        for part in range(2):
            for way in range(2):
                sends.append(
                    (ring_gives[part][way], lambda part=part, way=way: ring_copy(step, part, s, way).wait_send())
                )
        if s > 0:
            return
        for k in range(min(step, n_hist)):

            @pl.when((h == k) & root)
            def _():
                sxb[step, k] = sbuf[step, :, 0]

            away = (h == k) & (z != g)

            @pl.when(away)
            def _():
                sx_copy(step, k).start()

            sends.append((away, lambda k=k: sx_copy(step, k).wait_send()))

    def sums_before_last(step):
        begin = 0
        for end in range(max(1, sh - 2), sh):
            for s in range(begin, end):
                receive_s(step, s)
                store_s3(step, s)

            def one(t, begin=begin, end=end):
                product = dot_of(t, begin, end)
                acc[t] = acc[t] + product if begin else product

            loop(tt_all, one)
            begin = end
        receive_s(step, sh - 1)
        store_s3(step, sh - 1)

    def make_base(step):
        for k in range(min(step, n_hist)):

            @pl.when(h != k)
            def _():
                sx_copy(step, k).wait_recv()

            @pl.when(c == k % hp)
            def _():
                for d in range(1, hp):
                    sy_copy(step, k, d).start()

            store_l3(k + 1, norm * sxb[step, k, 1], -norm * sxb[step, k, 0])

        def one(tt):
            total = jnp.dot(l3[0], x3[step, tt], preferred_element_type=F32)
            for k in range(min(step, n_hist)):
                total += jnp.dot(l3[k + 1], x3[k + 1, tt], preferred_element_type=F32)
            real, imag = complex_of(total)
            base[tt, 0] = MIXING * real
            base[tt, 1] = MIXING * imag

        loop(sh, one)

    s_copy.wait()
    for s in range(sh):
        store_s3(0, s)
    pl.semaphore_wait(barrier, n_hist + 1)

    for step in range(last):
        if step > 0:
            sums_before_last(step)

        def first_link(tt, step=step):
            for d in range(1, hp):
                ex_copy(step, d, tt).wait_recv()
                own[step, tt] += exr[step, d, tt]

            @pl.when((z < g) & (z == 0))
            def _():
                for p in range(PIECES):
                    chain_copy(step, tt, p, True).start()

            @pl.when((z > g) & (z == nz - 1))
            def _():
                for p in range(PIECES):
                    chain_copy(step, tt, p, False).start()

        def products(tt, step=step):
            for d in range(1, hp):
                real, imag = term((c + d) % hp * sh + tt, step)
                exs[step, d, tt, 0] = real
                exs[step, d, tt, 1] = imag
                ex_copy(step, d, tt).start()
            real, imag = term(c * sh + tt, step)
            own[step, tt, 0] = real
            own[step, tt, 1] = imag
            pl.when(tt > 0)(lambda: first_link(tt - 1))

        loop(sh, products)
        first_link(sh - 1)
        for d in range(1, hp):
            sends.append((None, lambda d=d, step=step: loop(sh, lambda tt: ex_copy(step, d, tt).wait_send())))
        if step == 0:
            p_copy.wait()
            r_copy.wait()

        @pl.when(root)
        def _():
            if step == 0:
                store_l3(0, pin[0], pin[1])
                loop(sh, lambda tt: store_x3(0, tt, rin[0, c * sh + tt], rin[1, c * sh + tt]))
            make_base(step)

        def link(tt):
            for p in range(PIECES):
                part, at = piece(p)

                @pl.when((z > 0) & (z <= g))
                def _():
                    chain_copy(step, tt, p, True).wait_recv()
                    own[step, tt, part, at] += upb[step, tt, part, at]

                @pl.when((z < nz - 1) & (z >= g))
                def _():
                    chain_copy(step, tt, p, False).wait_recv()
                    own[step, tt, part, at] += dnb[step, tt, part, at]

                @pl.when((z < g) & (z > 0))
                def _():
                    chain_copy(step, tt, p, True).start()

                @pl.when((z > g) & (z < nz - 1))
                def _():
                    chain_copy(step, tt, p, False).start()

            @pl.when(root)
            def _():
                real = own[step, tt, 0] + base[tt, 0]
                imag = own[step, tt, 1] + base[tt, 1]
                modulus = real * real + imag * imag
                factor = -COUPLING * modulus / (1.0 + modulus)
                sbuf[step + 1, 0, tt] = factor * real
                sbuf[step + 1, 1, tt] = factor * imag
                for part, way in ((0, 0), (1, 1), (1, 0), (0, 1)):
                    ring_give(step + 1, tt, part, way)
                rows[step, 0, tt] = real
                rows[step, 1, tt] = imag
                store_x3(step + 1, tt, real, imag)

        loop(sh, link)
        for up, gives in ((True, z < g), (False, z > g)):
            for p in range(PIECES):
                sends.append(
                    (gives, lambda p=p, up=up, step=step: loop(sh, lambda tt: chain_copy(step, tt, p, up).wait_send()))
                )
        for k in range(min(step, n_hist)):
            for d in range(1, hp):
                sends.append((root & (c == k % hp), lambda k=k, d=d, step=step: sy_copy(step, k, d).wait_send()))

        @pl.when(root)
        def _():
            outb[step, :, pl.ds(c * sh, sh)] = rows[
                step, :, :, pl.ds(pl.multiple_of(h * band, band), band)
            ]
            loop(n_hist - 1, lambda e: band_copy(step, e + 1, c).start())

        sends.append(
            (root, lambda step=step: loop(n_hist - 1, lambda e: band_copy(step, e + 1, c).wait_send()))
        )

    sums_before_last(last)
    for k in range(min(last, n_hist)):
        for d in range(1, hp):
            sends.append((root & (c == k % hp), lambda k=k, d=d: sy_copy(last, k, d).wait_send()))
    pl.when(root)(lambda: make_base(last))
    for q in range(hp):

        def bands(tt, q=q):
            for part, value in enumerate(term(q * sh + tt, last)):
                for b in range(n_hist):
                    fin[q, b // hp, b % hp, tt, part] = value[b * band : (b + 1) * band]

        loop(sh, bands)

        @pl.when(root & (c == q))
        def _():
            def add(tt):
                for part in range(2):
                    for b in range(n_hist):
                        fin[q, b // hp, b % hp, tt, part] += base[tt, part, pl.ds(b * band, band)]

            loop(sh, add)

        for d in range(1, hp):
            fin_ex_copy(q, d).start()
            sends.append((None, lambda q=q, d=d: fin_ex_copy(q, d).wait_send()))

    for q in range(hp):
        for d in range(1, hp):
            fin_ex_copy(q, d).wait_recv()

        def both(zz, q=q):
            value = fin[q, zz, c]
            for d in range(1, hp):
                value += exf[q, d, zz]
            fsum[q, zz] = value

        loop(nz, both)
        for dist in range(nz - 1, 0, -1):
            for up in (True, False):
                zz = z + dist if up else z - dist
                on_way = zz < nz if up else zz >= 0
                first = z == 0 if up else z == nz - 1

                @pl.when(on_way)
                def _():
                    @pl.when(jnp.logical_not(first))
                    def _():
                        fin_chain_copy(q, zz, up).wait_recv()
                        fsum[q, zz] += (upf if up else dnf)[q, zz]

                    fin_chain_copy(q, zz, up).start()

                sends.append(
                    (on_way, lambda q=q, zz=zz, up=up: fin_chain_copy(q, zz, up).wait_send())
                )
    for q in range(hp):

        @pl.when(z > 0)
        def _():
            fin_chain_copy(q, z, True).wait_recv()
            fsum[q, z] += upf[q, z]

        @pl.when(z < nz - 1)
        def _():
            fin_chain_copy(q, z, False).wait_recv()
            fsum[q, z] += dnf[q, z]

        for tt in range(sh):
            for part in range(2):
                out_ref[last, part, q * sh + tt] = fsum[q, z, tt, part]

    for step in range(last):
        for sender in range(hp):

            @pl.when(h != g * hp + sender)
            def _():
                band_copy(step, 1, sender).wait_recv()

        out_ref[step] = outb[step]

    for gives, wait in sends:
        if gives is None:
            wait()
        else:
            pl.when(gives)(wait)


def per_device(history, self_energy, green_row, propagator):
    n_tgt, n_hist = lax.axis_size("tgt"), lax.axis_size("hist")
    _, sh, tt, n, _ = history.shape
    hp, band, last = n_hist // n_tgt, n // n_hist, STEPS - 1
    nz = n_hist // hp
    norm = float(sh * n_hist * n) ** (-0.5)
    vmem, sem = pltpu.VMEM, pltpu.SemaphoreType.DMA
    return pl.pallas_call(
        functools.partial(kernel, n_tgt, n_hist, norm),
        out_shape=jax.ShapeDtypeStruct((STEPS, 2, tt, band, n), F32),
        in_specs=[pl.BlockSpec(memory_space=pl.ANY)] * 4,
        out_specs=pl.BlockSpec(memory_space=pltpu.VMEM),
        scratch_shapes=[
            vmem((tt, 2, sh, n, n), F32),
            vmem((tt, 3 * sh * n, 2 * n), BF16),
            vmem((2 * n, 3 * sh * n), BF16),
            vmem((tt, 2 * n, 2 * n), F32),
            vmem((STEPS, 2, sh, n, n), F32),
            vmem((2, tt, n, n), F32),
            vmem((2, n, n), F32),
            vmem((last, hp, sh, 2, n, n), F32),
            vmem((last, hp, sh, 2, n, n), F32),
            vmem((last, sh, 2, n, n), F32),
            vmem((last, sh, 2, n, n), F32),
            vmem((last, sh, 2, n, n), F32),
            vmem((last, 2, sh, n, n), F32),
            vmem((STEPS, sh, 3 * n, 2 * n), BF16),
            vmem((sh, 2, n, n), F32),
            vmem((STEPS, STEPS, 2, n, n), F32),
            vmem((STEPS, 2 * n, 3 * n), BF16),
            vmem((last, 2, tt, band, n), F32),
            vmem((hp, nz, hp, sh, 2, band, n), F32),
            vmem((hp, hp, nz, sh, 2, band, n), F32),
            vmem((hp, nz, sh, 2, band, n), F32),
            vmem((hp, nz, sh, 2, band, n), F32),
            vmem((hp, nz, sh, 2, band, n), F32),
            sem((tt,)),
            sem((3,)),
            sem((last, hp, sh)),
            sem((last, hp, sh)),
            sem((last, sh, PIECES)),
            sem((last, sh, PIECES)),
            sem((last, sh, PIECES)),
            sem((STEPS, 2, 2, sh)),
            sem((STEPS, 2, sh)),
            sem((STEPS, STEPS)),
            sem((STEPS, STEPS, hp)),
            sem((STEPS, STEPS)),
            sem((last, n_hist)),
            sem((last, hp)),
            sem((hp, hp)),
            sem((hp, hp)),
            sem((hp, nz)),
            sem((hp, nz)),
            sem((hp, nz)),
        ],
        compiler_params=pltpu.CompilerParams(
            collective_id=0, has_side_effects=True, vmem_limit_bytes=56 * 2**20
        ),
    )(history, self_energy, green_row, propagator)


def solution(mesh):
    in_specs = (
        P(None, "hist", "tgt", None, None),
        P(None, "hist", None, None),
        P(None, "tgt", None, None),
        P(),
    )
    out_specs = P(None, None, "tgt", "hist", None)
    return jax.shard_map(
        per_device, mesh=mesh, in_specs=in_specs, out_specs=out_specs, check_vma=False
    )
```

```python
import functools

import jax
import jax.numpy as jnp
from jax import lax
from jax.experimental import pallas as pl
from jax.experimental.pallas import tpu as pltpu
from jax.sharding import PartitionSpec as P

STEPS = 4
COUPLING = 1.5
MIXING = 0.7
MESH = pl.DeviceIdType.MESH
CUTS = 2
PIECES = 4
F32, BF16 = jnp.float32, jnp.bfloat16


def split(value):
    high = value.astype(BF16)
    return high, (value - high.astype(F32)).astype(BF16)


def complex_of(product):
    n = product.shape[0] // 2
    return product[:n, :n] - product[n:, n:], product[:n, n:] + product[n:, :n]


def snake(index):
    q, r = index // 2, index % 2
    return 2 * q + r + (q % 2) * (1 - 2 * r)


def kernel(
    n_tgt, n_hist, norm,
    h_hbm, s_hbm, r_hbm, p_hbm, out_ref,
    hst, h3, s3, acc, sbuf, rin, pin, exs, exr, own, upb, dnb, rows, x3, base, sxb, l3, outb,
    fin, exf, fsum, upf, dnf,
    h_sem, in_sem, ex_s, ex_r, ch_s, up_r, dn_r, rg_s, rg_r, sx_s, sy_s, sx_r, bd_s, bd_r,
    fx_s, fx_r, fc_s, fu_r, fd_r,
):
    _, sh, tt_all, n, _ = h_hbm.shape
    hp = n_hist // n_tgt
    nz = n_hist // hp
    band = n // n_hist
    depth = sh * n
    g, h = lax.axis_index("tgt"), lax.axis_index("hist")
    z, c = h // hp, h % hp
    root = z == g
    pos = snake(g)
    rel = (pos - snake(z) + n_tgt) % n_tgt
    ahead, behind = snake((pos + 1) % n_tgt), snake((pos + n_tgt - 1) % n_tgt)
    last = STEPS - 1
    sends, bands_sent, older = [], [], []

    def remote(src, dst, send_sem, recv_sem, tgt, hist):
        return pltpu.make_async_remote_copy(
            src_ref=src, dst_ref=dst, send_sem=send_sem, recv_sem=recv_sem,
            device_id={"tgt": tgt, "hist": hist}, device_id_type=MESH,
        )

    def loop(count, body):
        lax.fori_loop(0, count, lambda i, _: (body(i), None)[1], None)

    def h_copy(t):
        return pltpu.make_async_copy(h_hbm.at[:, :, t], hst.at[t], h_sem.at[t])

    s_copy = pltpu.make_async_copy(s_hbm, sbuf.at[0], in_sem.at[0])
    p_copy = pltpu.make_async_copy(p_hbm, pin, in_sem.at[1])
    r_copy = pltpu.make_async_copy(r_hbm, rin, in_sem.at[2])
    s_copy.start()
    for d in [*range(1, hp), 0]:
        loop(sh, lambda t, d=d: h_copy((c + d) % hp * sh + t).start())
    p_copy.start()
    r_copy.start()

    barrier = pltpu.get_barrier_semaphore()
    for e in range(1, n_hist):
        pl.semaphore_signal(
            barrier, inc=1, device_id={"tgt": g, "hist": (h + e) % n_hist}, device_id_type=MESH
        )
    for near in (ahead, behind):
        pl.semaphore_signal(barrier, inc=1, device_id={"tgt": near, "hist": h}, device_id_type=MESH)

    def store_x3(slot, tt, real, imag):
        for at, value in ((0, real), (n, imag)):
            high, low = split(value)
            cols = pl.ds(at, n)
            x3[slot, tt, pl.ds(0, n), cols] = high
            x3[slot, tt, pl.ds(n, n), cols] = low
            x3[slot, tt, pl.ds(2 * n, n), cols] = high

    def store_l3(slot, real, imag):
        for at, value in ((0, real), (n, imag)):
            high, low = split(value)
            l3[slot, pl.ds(at, n), pl.ds(0, n)] = high
            l3[slot, pl.ds(at, n), pl.ds(n, n)] = high
            l3[slot, pl.ds(at, n), pl.ds(2 * n, n)] = low

    half = sh // 2
    width = 3 * n

    def store_s3(step, s):
        for part in range(2):
            high, low = split(sbuf[step, part, s])
            r = pl.ds(part * n, n)
            s3[r, pl.ds(s * width, n)] = high
            s3[r, pl.ds(s * width + n, n)] = high
            s3[r, pl.ds(s * width + 2 * n, n)] = low
        if step > 0 and s == 0:

            @pl.when(h < step)
            def _():
                s3[:, pl.ds(0, width)] = jnp.zeros((2 * n, width), BF16)

    def store_h3(t):
        h_copy(t).wait()
        for s in range(sh):
            for part in range(2):
                high, low = split(hst[t, part, s])
                cols = pl.ds(part * n, n)
                h3[t, pl.ds(s * width, n), cols] = high
                h3[t, pl.ds(s * width + n, n), cols] = low
                h3[t, pl.ds(s * width + 2 * n, n), cols] = high

    def dot_of(t, begin, end):
        at = pl.ds(begin * width, (end - begin) * width)
        return jnp.dot(s3[:, at], h3[t, at, :], preferred_element_type=F32)

    def term(t, step):
        if step == 0:
            store_h3(t)
            product = dot_of(t, 0, sh)
        else:
            product = acc[t] + dot_of(t, half, sh)
        real, imag = complex_of(product)
        return (MIXING * norm) * imag, (-MIXING * norm) * real

    def ex_copy(step, d, tt):
        return remote(
            exs.at[step, d, tt], exr.at[step, d, tt], ex_s.at[step, d, tt], ex_r.at[step, d, tt],
            g, z * hp + (c + d) % hp,
        )

    def piece(p):
        per_part = PIECES // 2
        return p // per_part, pl.ds(p % per_part * (n // per_part), n // per_part)

    def chain_copy(step, tt, p, up):
        part, at = piece(p)
        return remote(
            own.at[step, tt, part, at], (upb if up else dnb).at[step, tt, part, at],
            ch_s.at[step, tt, p], (up_r if up else dn_r).at[step, tt, p],
            g, h + hp if up else h - hp,
        )

    def ring_copy(step, part, s, way):
        ref = sbuf.at[step, part, s]
        return remote(
            ref, ref, rg_s.at[step, way, part, s], rg_r.at[step, part, s],
            behind if way else ahead, h,
        )

    reach = (n_tgt // 2, n_tgt // 2 - 1)
    ring_gives = [(rel < reach[p], (rel == 0) | (rel >= reach[p] + 2)) for p in range(2)]

    def ring_give(step, s, part, way):
        @pl.when(ring_gives[part][way])
        def _():
            ring_copy(step, part, s, way).start()

    def sx_copy(step, k):
        return remote(
            sbuf.at[step, :, 0], sxb.at[step, k], sx_s.at[step, k], sx_r.at[step, k],
            g, g * hp + k % hp,
        )

    def sy_copy(step, k, d):
        return remote(
            sxb.at[step, k], sxb.at[step, k], sy_s.at[step, k, d], sx_r.at[step, k],
            g, z * hp + (c + d) % hp,
        )

    def band_copy(step, e, sender):
        to = (h + e) % n_hist
        return remote(
            rows.at[step, :, :, pl.ds(pl.multiple_of(to * band, band), band)],
            outb.at[step, :, pl.ds(sender * sh, sh)], bd_s.at[step, e], bd_r.at[step, sender],
            g, to,
        )

    def fin_ex_copy(q, d):
        to = (c + d) % hp
        return remote(
            fin.at[q, :, to], exf.at[q, d], fx_s.at[q, d], fx_r.at[q, d], g, z * hp + to
        )

    def fin_chain_copy(q, zz, up):
        return remote(
            fsum.at[q, zz], (upf if up else dnf).at[q, zz], fc_s.at[q, zz],
            (fu_r if up else fd_r).at[q, zz], g, h + hp if up else h - hp,
        )

    def receive_s(step, s):
        @pl.when(rel > 0)
        def _():
            for part in range(2):
                ring_copy(step, part, s, 0).wait_recv()
                ring_give(step, s, part, 0)
                ring_give(step, s, part, 1)

        for part in range(2):
            for way in range(2):
                sends.append(
                    (ring_gives[part][way], lambda part=part, way=way: ring_copy(step, part, s, way).wait_send())
                )
        if s > 0:
            return
        for k in range(min(step, n_hist)):

            @pl.when((h == k) & root)
            def _():
                sxb[step, k] = sbuf[step, :, 0]

            away = (h == k) & (z != g)

            @pl.when(away)
            def _():
                sx_copy(step, k).start()

            sends.append((away, lambda k=k: sx_copy(step, k).wait_send()))

    def first_sums(step):
        for s in range(half):
            receive_s(step, s)
            store_s3(step, s)

        def one(t):
            acc[t] = dot_of(t, 0, half)

        loop(tt_all, one)
        for s in range(half, sh):
            receive_s(step, s)
        for s in range(half, sh):
            store_s3(step, s)

    def flush(waits):
        for gives, wait in waits:
            if gives is None:
                wait()
            else:
                pl.when(gives)(wait)
        waits.clear()

    def make_base(step):
        for k in range(min(step, n_hist)):

            @pl.when(h != k)
            def _():
                sx_copy(step, k).wait_recv()

            @pl.when(c == k % hp)
            def _():
                for d in range(1, hp):
                    sy_copy(step, k, d).start()

            store_l3(k + 1, norm * sxb[step, k, 1], -norm * sxb[step, k, 0])

        def one(tt):
            total = jnp.dot(l3[0], x3[step, tt], preferred_element_type=F32)
            for k in range(min(step, n_hist)):
                total += jnp.dot(l3[k + 1], x3[k + 1, tt], preferred_element_type=F32)
            real, imag = complex_of(total)
            base[tt, 0] = MIXING * real
            base[tt, 1] = MIXING * imag

        loop(sh, one)

    s_copy.wait()
    for s in range(sh):
        store_s3(0, s)
    pl.semaphore_wait(barrier, n_hist + 1)

    for step in range(last):
        if step > 0:
            flush(sends)
            flush(older)
            older, bands_sent = bands_sent, []
            first_sums(step)

        def first_link(tt, step=step):
            for d in range(1, hp):
                ex_copy(step, d, tt).wait_recv()
                own[step, tt] += exr[step, d, tt]

            @pl.when((z < g) & (z == 0))
            def _():
                for p in range(PIECES):
                    chain_copy(step, tt, p, True).start()

            @pl.when((z > g) & (z == nz - 1))
            def _():
                for p in range(PIECES):
                    chain_copy(step, tt, p, False).start()

        def products(tt, step=step):
            for d in range(1, hp):
                real, imag = term((c + d) % hp * sh + tt, step)
                exs[step, d, tt, 0] = real
                exs[step, d, tt, 1] = imag
                ex_copy(step, d, tt).start()
            real, imag = term(c * sh + tt, step)
            own[step, tt, 0] = real
            own[step, tt, 1] = imag
            pl.when(tt > 0)(lambda: first_link(tt - 1))

        loop(sh, products)
        first_link(sh - 1)
        for d in range(1, hp):
            sends.append((None, lambda d=d, step=step: loop(sh, lambda tt: ex_copy(step, d, tt).wait_send())))
        if step == 0:
            p_copy.wait()
            r_copy.wait()

        @pl.when(root)
        def _():
            if step == 0:
                store_l3(0, pin[0], pin[1])
                loop(sh, lambda tt: store_x3(0, tt, rin[0, c * sh + tt], rin[1, c * sh + tt]))
            make_base(step)

        def link(tt):
            for p in range(PIECES):
                part, at = piece(p)

                @pl.when((z > 0) & (z <= g))
                def _():
                    chain_copy(step, tt, p, True).wait_recv()
                    own[step, tt, part, at] += upb[step, tt, part, at]

                @pl.when((z < nz - 1) & (z >= g))
                def _():
                    chain_copy(step, tt, p, False).wait_recv()
                    own[step, tt, part, at] += dnb[step, tt, part, at]

                @pl.when((z < g) & (z > 0))
                def _():
                    chain_copy(step, tt, p, True).start()

                @pl.when((z > g) & (z < nz - 1))
                def _():
                    chain_copy(step, tt, p, False).start()

            @pl.when(root)
            def _():
                real = own[step, tt, 0] + base[tt, 0]
                imag = own[step, tt, 1] + base[tt, 1]
                modulus = real * real + imag * imag
                factor = -COUPLING * modulus / (1.0 + modulus)
                sbuf[step + 1, 0, tt] = factor * real
                sbuf[step + 1, 1, tt] = factor * imag
                for part, way in ((0, 0), (1, 1), (1, 0), (0, 1)):
                    ring_give(step + 1, tt, part, way)
                rows[step, 0, tt] = real
                rows[step, 1, tt] = imag
                store_x3(step + 1, tt, real, imag)

        loop(sh, link)
        for up, gives in ((True, z < g), (False, z > g)):
            for p in range(PIECES):
                sends.append(
                    (gives, lambda p=p, up=up, step=step: loop(sh, lambda tt: chain_copy(step, tt, p, up).wait_send()))
                )
        for k in range(min(step, n_hist)):
            for d in range(1, hp):
                sends.append((root & (c == k % hp), lambda k=k, d=d, step=step: sy_copy(step, k, d).wait_send()))

        @pl.when(root)
        def _():
            outb[step, :, pl.ds(c * sh, sh)] = rows[
                step, :, :, pl.ds(pl.multiple_of(h * band, band), band)
            ]
            loop(n_hist - 1, lambda e: band_copy(step, e + 1, c).start())

        bands_sent.append(
            (root, lambda step=step: loop(n_hist - 1, lambda e: band_copy(step, e + 1, c).wait_send()))
        )

    flush(sends)
    flush(older)
    first_sums(last)
    for k in range(min(last, n_hist)):
        for d in range(1, hp):
            sends.append((root & (c == k % hp), lambda k=k, d=d: sy_copy(last, k, d).wait_send()))
    pl.when(root)(lambda: make_base(last))
    n_cut, su = fin.shape[0], fin.shape[3]
    per_core = n_cut // hp

    def far(u, go):
        for dist in range(nz - 1, 0, -1):
            for up in (True, False):
                zz = z + dist if up else z - dist
                on_way = zz < nz if up else zz >= 0
                go(u, zz, up, on_way, z == 0 if up else z == nz - 1)

    def far_first(u, zz, up, on_way, first):
        @pl.when(on_way & first)
        def _():
            fin_chain_copy(u, zz, up).start()

    def far_next(u, zz, up, on_way, first):
        @pl.when(on_way & jnp.logical_not(first))
        def _():
            fin_chain_copy(u, zz, up).wait_recv()
            fsum[u, zz] += (upf if up else dnf)[u, zz]
            fin_chain_copy(u, zz, up).start()

        sends.append((on_way, lambda: fin_chain_copy(u, zz, up).wait_send()))

    def of_pair(u):
        for d in range(1, hp):
            fin_ex_copy(u, d).wait_recv()

        def both(zz):
            value = fin[u, zz, c]
            for d in range(1, hp):
                value += exf[u, d, zz]
            fsum[u, zz] = value

        loop(nz, both)
        far(u, far_first)

    for u in range(n_cut):

        def bands(i, u=u):
            for part, value in enumerate(term(u * su + i, last)):
                for b in range(n_hist):
                    fin[u, b // hp, b % hp, i, part] = value[b * band : (b + 1) * band]

        loop(su, bands)

        @pl.when(root & (c == u // per_core))
        def _():
            def add(i):
                for part in range(2):
                    for b in range(n_hist):
                        fin[u, b // hp, b % hp, i, part] += base[
                            u % per_core * su + i, part, pl.ds(b * band, band)
                        ]

            loop(su, add)

        for d in range(1, hp):
            fin_ex_copy(u, d).start()
            sends.append((None, lambda u=u, d=d: fin_ex_copy(u, d).wait_send()))
        if u > 0:
            of_pair(u - 1)
    of_pair(n_cut - 1)

    for u in range(n_cut):
        far(u, far_next)
    for step in range(last):
        for sender in range(hp):

            @pl.when(h != g * hp + sender)
            def _():
                band_copy(step, 1, sender).wait_recv()

        out_ref[step] = outb[step]
    for u in range(n_cut):

        @pl.when(z > 0)
        def _():
            fin_chain_copy(u, z, True).wait_recv()
            fsum[u, z] += upf[u, z]

        @pl.when(z < nz - 1)
        def _():
            fin_chain_copy(u, z, False).wait_recv()
            fsum[u, z] += dnf[u, z]

        for i in range(su):
            for part in range(2):
                out_ref[last, part, u * su + i] = fsum[u, z, i, part]

    flush(bands_sent)
    flush(sends)


def per_device(history, self_energy, green_row, propagator):
    n_tgt, n_hist = lax.axis_size("tgt"), lax.axis_size("hist")
    _, sh, tt, n, _ = history.shape
    hp, band, last = n_hist // n_tgt, n // n_hist, STEPS - 1
    nz = n_hist // hp
    norm = float(sh * n_hist * n) ** (-0.5)
    n_cut = hp * CUTS
    su = tt // n_cut
    vmem, sem = pltpu.VMEM, pltpu.SemaphoreType.DMA
    return pl.pallas_call(
        functools.partial(kernel, n_tgt, n_hist, norm),
        out_shape=jax.ShapeDtypeStruct((STEPS, 2, tt, band, n), F32),
        in_specs=[pl.BlockSpec(memory_space=pl.ANY)] * 4,
        out_specs=pl.BlockSpec(memory_space=pltpu.VMEM),
        scratch_shapes=[
            vmem((tt, 2, sh, n, n), F32),
            vmem((tt, 3 * sh * n, 2 * n), BF16),
            vmem((2 * n, 3 * sh * n), BF16),
            vmem((tt, 2 * n, 2 * n), F32),
            vmem((STEPS, 2, sh, n, n), F32),
            vmem((2, tt, n, n), F32),
            vmem((2, n, n), F32),
            vmem((last, hp, sh, 2, n, n), F32),
            vmem((last, hp, sh, 2, n, n), F32),
            vmem((last, sh, 2, n, n), F32),
            vmem((last, sh, 2, n, n), F32),
            vmem((last, sh, 2, n, n), F32),
            vmem((last, 2, sh, n, n), F32),
            vmem((STEPS, sh, 3 * n, 2 * n), BF16),
            vmem((sh, 2, n, n), F32),
            vmem((STEPS, STEPS, 2, n, n), F32),
            vmem((STEPS, 2 * n, 3 * n), BF16),
            vmem((last, 2, tt, band, n), F32),
            vmem((n_cut, nz, hp, su, 2, band, n), F32),
            vmem((n_cut, hp, nz, su, 2, band, n), F32),
            vmem((n_cut, nz, su, 2, band, n), F32),
            vmem((n_cut, nz, su, 2, band, n), F32),
            vmem((n_cut, nz, su, 2, band, n), F32),
            sem((tt,)),
            sem((3,)),
            sem((last, hp, sh)),
            sem((last, hp, sh)),
            sem((last, sh, PIECES)),
            sem((last, sh, PIECES)),
            sem((last, sh, PIECES)),
            sem((STEPS, 2, 2, sh)),
            sem((STEPS, 2, sh)),
            sem((STEPS, STEPS)),
            sem((STEPS, STEPS, hp)),
            sem((STEPS, STEPS)),
            sem((last, n_hist)),
            sem((last, hp)),
            sem((n_cut, hp)),
            sem((n_cut, hp)),
            sem((n_cut, nz)),
            sem((n_cut, nz)),
            sem((n_cut, nz)),
        ],
        compiler_params=pltpu.CompilerParams(
            collective_id=0, has_side_effects=True, vmem_limit_bytes=56 * 2**20
        ),
    )(history, self_energy, green_row, propagator)


def solution(mesh):
    in_specs = (
        P(None, "hist", "tgt", None, None),
        P(None, "hist", None, None),
        P(None, "tgt", None, None),
        P(),
    )
    out_specs = P(None, None, "tgt", "hist", None)
    return jax.shard_map(
        per_device, mesh=mesh, in_specs=in_specs, out_specs=out_specs, check_vma=False
    )
```

```python
import functools

import jax
import jax.numpy as jnp
from jax import lax
from jax.experimental import pallas as pl
from jax.experimental.pallas import tpu as pltpu
from jax.sharding import PartitionSpec as P

STEPS = 4
COUPLING = 1.5
MIXING = 0.7
MESH = pl.DeviceIdType.MESH
CUTS = 2
PIECES = 4
F32, BF16 = jnp.float32, jnp.bfloat16


def split(value):
    high = value.astype(BF16)
    return high, (value - high.astype(F32)).astype(BF16)


def complex_of(product):
    n = product.shape[0] // 2
    return product[:n, :n] - product[n:, n:], product[:n, n:] + product[n:, :n]


def snake(index):
    q, r = index // 2, index % 2
    return 2 * q + r + (q % 2) * (1 - 2 * r)


def kernel(
    n_tgt, n_hist, norm,
    h_hbm, s_hbm, r_hbm, p_hbm, out_ref,
    hst, h3, s3, acc, sbuf, rin, pin, exs, exr, own, upb, dnb, rows, x3, base, sxb, l3, outb,
    fin, exf, fsum, upf, dnf,
    h_sem, in_sem, ex_s, ex_r, ch_s, up_r, dn_r, rg_s, rg_r, sx_s, sy_s, sx_r, bd_s, bd_r,
    fx_s, fx_r, fc_s, fu_r, fd_r,
):
    _, sh, tt_all, n, _ = h_hbm.shape
    hp = n_hist // n_tgt
    nz = n_hist // hp
    band = n // n_hist
    depth = sh * n
    g, h = lax.axis_index("tgt"), lax.axis_index("hist")
    z, c = h // hp, h % hp
    root = z == g
    pos = snake(g)
    rel = (pos - snake(z) + n_tgt) % n_tgt
    ahead, behind = snake((pos + 1) % n_tgt), snake((pos + n_tgt - 1) % n_tgt)
    last = STEPS - 1
    sends, bands_sent, older = [], [], []

    def remote(src, dst, send_sem, recv_sem, tgt, hist):
        return pltpu.make_async_remote_copy(
            src_ref=src, dst_ref=dst, send_sem=send_sem, recv_sem=recv_sem,
            device_id={"tgt": tgt, "hist": hist}, device_id_type=MESH,
        )

    def loop(count, body):
        lax.fori_loop(0, count, lambda i, _: (body(i), None)[1], None)

    def h_copy(t):
        return pltpu.make_async_copy(h_hbm.at[:, :, t], hst.at[t], h_sem.at[t])

    s_copy = pltpu.make_async_copy(s_hbm, sbuf.at[0], in_sem.at[0])
    p_copy = pltpu.make_async_copy(p_hbm, pin, in_sem.at[1])
    r_copy = pltpu.make_async_copy(r_hbm, rin, in_sem.at[2])
    s_copy.start()
    for d in [*range(1, hp), 0]:
        loop(sh, lambda t, d=d: h_copy((c + d) % hp * sh + t).start())
    p_copy.start()
    r_copy.start()

    barrier = pltpu.get_barrier_semaphore()
    for e in range(1, n_hist):
        pl.semaphore_signal(
            barrier, inc=1, device_id={"tgt": g, "hist": (h + e) % n_hist}, device_id_type=MESH
        )
    for near in (ahead, behind):
        pl.semaphore_signal(barrier, inc=1, device_id={"tgt": near, "hist": h}, device_id_type=MESH)

    def store_x3(slot, tt, real, imag):
        for at, value in ((0, real), (n, imag)):
            high, low = split(value)
            cols = pl.ds(at, n)
            x3[slot, tt, pl.ds(0, n), cols] = high
            x3[slot, tt, pl.ds(n, n), cols] = low
            x3[slot, tt, pl.ds(2 * n, n), cols] = high

    def store_l3(slot, real, imag):
        for at, value in ((0, real), (n, imag)):
            high, low = split(value)
            l3[slot, pl.ds(at, n), pl.ds(0, n)] = high
            l3[slot, pl.ds(at, n), pl.ds(n, n)] = high
            l3[slot, pl.ds(at, n), pl.ds(2 * n, n)] = low

    half = sh // 2
    width = 3 * n

    def store_s3(step, s):
        for part in range(2):
            high, low = split(sbuf[step, part, s])
            r = pl.ds(part * n, n)
            s3[r, pl.ds(s * width, n)] = high
            s3[r, pl.ds(s * width + n, n)] = high
            s3[r, pl.ds(s * width + 2 * n, n)] = low
        if step > 0 and s == 0:

            @pl.when(h < step)
            def _():
                s3[:, pl.ds(0, width)] = jnp.zeros((2 * n, width), BF16)

    def store_h3(t):
        h_copy(t).wait()
        for s in range(sh):
            for part in range(2):
                high, low = split(hst[t, part, s])
                cols = pl.ds(part * n, n)
                h3[t, pl.ds(s * width, n), cols] = high
                h3[t, pl.ds(s * width + n, n), cols] = low
                h3[t, pl.ds(s * width + 2 * n, n), cols] = high

    def dot_of(t, begin, end):
        at = pl.ds(begin * width, (end - begin) * width)
        return jnp.dot(s3[:, at], h3[t, at, :], preferred_element_type=F32)

    def term(t, step):
        if step == 0:
            store_h3(t)
            product = dot_of(t, 0, sh)
        else:
            product = acc[t] + dot_of(t, half, sh)
        real, imag = complex_of(product)
        return (MIXING * norm) * imag, (-MIXING * norm) * real

    def ex_copy(step, d, tt):
        return remote(
            exs.at[step, d, tt], exr.at[step, d, tt], ex_s.at[step, d, tt], ex_r.at[step, d, tt],
            g, z * hp + (c + d) % hp,
        )

    def piece(p):
        return pl.ds(p * (n // PIECES), n // PIECES)

    def chain_copy(step, tt, p, up):
        at = piece(p)
        return remote(
            own.at[step, tt, :, at], (upb if up else dnb).at[step, tt, :, at],
            ch_s.at[step, tt, p], (up_r if up else dn_r).at[step, tt, p],
            g, h + hp if up else h - hp,
        )

    def ring_copy(step, p, s, way):
        ref = sbuf.at[step, :, s, piece(p)]
        return remote(
            ref, ref, rg_s.at[step, way, p, s], rg_r.at[step, p, s],
            behind if way else ahead, h,
        )

    reach = (n_tgt // 2, n_tgt // 2 - 1)
    ring_gives = [(rel < reach[p], (rel == 0) | (rel >= reach[p] + 2)) for p in range(2)] * (PIECES // 2)

    def ring_give(step, s, p):
        for way in (p % 2, 1 - p % 2):

            @pl.when(ring_gives[p][way])
            def _():
                ring_copy(step, p, s, way).start()

    def sx_copy(step, k):
        return remote(
            sbuf.at[step, :, 0], sxb.at[step, k], sx_s.at[step, k], sx_r.at[step, k],
            g, g * hp + k % hp,
        )

    def sy_copy(step, k, d):
        return remote(
            sxb.at[step, k], sxb.at[step, k], sy_s.at[step, k, d], sx_r.at[step, k],
            g, z * hp + (c + d) % hp,
        )

    def band_copy(step, e, sender):
        to = (h + e) % n_hist
        return remote(
            rows.at[step, :, :, pl.ds(pl.multiple_of(to * band, band), band)],
            outb.at[step, :, pl.ds(sender * sh, sh)], bd_s.at[step, e], bd_r.at[step, sender],
            g, to,
        )

    def fin_ex_copy(q, d):
        to = (c + d) % hp
        return remote(
            fin.at[q, :, to], exf.at[q, d], fx_s.at[q, d], fx_r.at[q, d], g, z * hp + to
        )

    def fin_chain_copy(q, zz, up):
        return remote(
            fsum.at[q, zz], (upf if up else dnf).at[q, zz], fc_s.at[q, zz],
            (fu_r if up else fd_r).at[q, zz], g, h + hp if up else h - hp,
        )

    def receive_s(step, s):
        @pl.when(rel > 0)
        def _():
            for p in range(PIECES):
                ring_copy(step, p, s, 0).wait_recv()
                ring_give(step, s, p)

        for p in range(PIECES):
            for way in range(2):
                sends.append(
                    (ring_gives[p][way], lambda p=p, way=way: ring_copy(step, p, s, way).wait_send())
                )
        if s > 0:
            return
        for k in range(min(step, n_hist)):

            @pl.when((h == k) & root)
            def _():
                sxb[step, k] = sbuf[step, :, 0]

            away = (h == k) & (z != g)

            @pl.when(away)
            def _():
                sx_copy(step, k).start()

            sends.append((away, lambda k=k: sx_copy(step, k).wait_send()))

    def first_sums(step):
        for s in range(half):
            receive_s(step, s)
            store_s3(step, s)

        def one(i):
            pair = [dot_of(2 * i + j, 0, half) for j in range(2)]
            for j in range(2):
                acc[2 * i + j] = pair[j]

        loop(tt_all // 2, one)
        for s in range(half, sh):
            receive_s(step, s)
        for s in range(half, sh):
            store_s3(step, s)

    def flush(waits):
        for gives, wait in waits:
            if gives is None:
                wait()
            else:
                pl.when(gives)(wait)
        waits.clear()

    def make_base(step):
        for k in range(min(step, n_hist)):

            @pl.when(h != k)
            def _():
                sx_copy(step, k).wait_recv()

            @pl.when(c == k % hp)
            def _():
                for d in range(1, hp):
                    sy_copy(step, k, d).start()

            store_l3(k + 1, norm * sxb[step, k, 1], -norm * sxb[step, k, 0])

        def one(tt):
            total = jnp.dot(l3[0], x3[step, tt], preferred_element_type=F32)
            for k in range(min(step, n_hist)):
                total += jnp.dot(l3[k + 1], x3[k + 1, tt], preferred_element_type=F32)
            real, imag = complex_of(total)
            base[tt, 0] = MIXING * real
            base[tt, 1] = MIXING * imag

        loop(sh, one)

    s_copy.wait()
    for s in range(sh):
        store_s3(0, s)
    pl.semaphore_wait(barrier, n_hist + 1)

    for step in range(last):
        if step > 0:
            flush(sends)
            flush(older)
            older, bands_sent = bands_sent, []
            first_sums(step)

        def first_link(tt, step=step):
            for d in range(1, hp):
                ex_copy(step, d, tt).wait_recv()
                own[step, tt] += exr[step, d, tt]

            @pl.when((z < g) & (z == 0))
            def _():
                for p in range(PIECES):
                    chain_copy(step, tt, p, True).start()

            @pl.when((z > g) & (z == nz - 1))
            def _():
                for p in range(PIECES):
                    chain_copy(step, tt, p, False).start()

        def products(tt, step=step):
            terms = [term((c + d) % hp * sh + tt, step) for d in [*range(1, hp), 0]]
            for d in range(1, hp):
                exs[step, d, tt, 0], exs[step, d, tt, 1] = terms[d - 1]
                ex_copy(step, d, tt).start()
            own[step, tt, 0], own[step, tt, 1] = terms[hp - 1]
            pl.when(tt > 0)(lambda: first_link(tt - 1))

        loop(sh, products)
        first_link(sh - 1)
        for d in range(1, hp):
            sends.append((None, lambda d=d, step=step: loop(sh, lambda tt: ex_copy(step, d, tt).wait_send())))
        if step == 0:
            p_copy.wait()
            r_copy.wait()

        @pl.when(root)
        def _():
            if step == 0:
                store_l3(0, pin[0], pin[1])
                loop(sh, lambda tt: store_x3(0, tt, rin[0, c * sh + tt], rin[1, c * sh + tt]))
            make_base(step)

        def link(tt):
            for p in range(PIECES):
                at = piece(p)

                @pl.when((z > 0) & (z <= g))
                def _():
                    chain_copy(step, tt, p, True).wait_recv()
                    own[step, tt, :, at] += upb[step, tt, :, at]

                @pl.when((z < nz - 1) & (z >= g))
                def _():
                    chain_copy(step, tt, p, False).wait_recv()
                    own[step, tt, :, at] += dnb[step, tt, :, at]

                @pl.when((z < g) & (z > 0))
                def _():
                    chain_copy(step, tt, p, True).start()

                @pl.when((z > g) & (z < nz - 1))
                def _():
                    chain_copy(step, tt, p, False).start()

                @pl.when(root)
                def _():
                    real = own[step, tt, 0, at] + base[tt, 0, at]
                    imag = own[step, tt, 1, at] + base[tt, 1, at]
                    modulus = real * real + imag * imag
                    factor = -COUPLING * modulus / (1.0 + modulus)
                    sbuf[step + 1, 0, tt, at] = factor * real
                    sbuf[step + 1, 1, tt, at] = factor * imag
                    ring_give(step + 1, tt, p)
                    rows[step, 0, tt, at] = real
                    rows[step, 1, tt, at] = imag

            @pl.when(root)
            def _():
                store_x3(step + 1, tt, rows[step, 0, tt], rows[step, 1, tt])

        loop(sh, link)
        for up, gives in ((True, z < g), (False, z > g)):
            for p in range(PIECES):
                sends.append(
                    (gives, lambda p=p, up=up, step=step: loop(sh, lambda tt: chain_copy(step, tt, p, up).wait_send()))
                )
        for k in range(min(step, n_hist)):
            for d in range(1, hp):
                sends.append((root & (c == k % hp), lambda k=k, d=d, step=step: sy_copy(step, k, d).wait_send()))

        @pl.when(root)
        def _():
            outb[step, :, pl.ds(c * sh, sh)] = rows[
                step, :, :, pl.ds(pl.multiple_of(h * band, band), band)
            ]
            loop(n_hist - 1, lambda e: band_copy(step, e + 1, c).start())

        bands_sent.append(
            (root, lambda step=step: loop(n_hist - 1, lambda e: band_copy(step, e + 1, c).wait_send()))
        )

    flush(sends)
    flush(older)
    first_sums(last)
    for k in range(min(last, n_hist)):
        for d in range(1, hp):
            sends.append((root & (c == k % hp), lambda k=k, d=d: sy_copy(last, k, d).wait_send()))
    pl.when(root)(lambda: make_base(last))
    n_cut, su = fin.shape[0], fin.shape[3]
    per_core = n_cut // hp

    def far(u, go):
        for dist in range(nz - 1, 0, -1):
            for up in (True, False):
                zz = z + dist if up else z - dist
                on_way = zz < nz if up else zz >= 0
                go(u, zz, up, on_way, z == 0 if up else z == nz - 1)

    def far_first(u, zz, up, on_way, first):
        @pl.when(on_way & first)
        def _():
            fin_chain_copy(u, zz, up).start()

    def far_next(u, zz, up, on_way, first):
        @pl.when(on_way & jnp.logical_not(first))
        def _():
            fin_chain_copy(u, zz, up).wait_recv()
            fsum[u, zz] += (upf if up else dnf)[u, zz]
            fin_chain_copy(u, zz, up).start()

        sends.append((on_way, lambda: fin_chain_copy(u, zz, up).wait_send()))

    def of_pair(u):
        for d in range(1, hp):
            fin_ex_copy(u, d).wait_recv()

        def both(zz):
            value = fin[u, zz, c]
            for d in range(1, hp):
                value += exf[u, d, zz]
            fsum[u, zz] = value

        loop(nz, both)
        far(u, far_first)

    for u in range(n_cut):

        def bands(i, u=u):
            for part, value in enumerate(term(u * su + i, last)):
                for b in range(n_hist):
                    fin[u, b // hp, b % hp, i, part] = value[b * band : (b + 1) * band]

        loop(su, bands)

        @pl.when(root & (c == u // per_core))
        def _():
            def add(i):
                for part in range(2):
                    for b in range(n_hist):
                        fin[u, b // hp, b % hp, i, part] += base[
                            u % per_core * su + i, part, pl.ds(b * band, band)
                        ]

            loop(su, add)

        for d in range(1, hp):
            fin_ex_copy(u, d).start()
            sends.append((None, lambda u=u, d=d: fin_ex_copy(u, d).wait_send()))
        if u > 0:
            of_pair(u - 1)
    of_pair(n_cut - 1)

    for u in range(n_cut):
        far(u, far_next)
    for step in range(last):
        for sender in range(hp):

            @pl.when(h != g * hp + sender)
            def _():
                band_copy(step, 1, sender).wait_recv()

        out_ref[step] = outb[step]
    for u in range(n_cut):

        @pl.when(z > 0)
        def _():
            fin_chain_copy(u, z, True).wait_recv()
            fsum[u, z] += upf[u, z]

        @pl.when(z < nz - 1)
        def _():
            fin_chain_copy(u, z, False).wait_recv()
            fsum[u, z] += dnf[u, z]

        for i in range(su):
            for part in range(2):
                out_ref[last, part, u * su + i] = fsum[u, z, i, part]

    flush(bands_sent)
    flush(sends)


def per_device(history, self_energy, green_row, propagator):
    n_tgt, n_hist = lax.axis_size("tgt"), lax.axis_size("hist")
    _, sh, tt, n, _ = history.shape
    hp, band, last = n_hist // n_tgt, n // n_hist, STEPS - 1
    nz = n_hist // hp
    norm = float(sh * n_hist * n) ** (-0.5)
    n_cut = hp * CUTS
    su = tt // n_cut
    vmem, sem = pltpu.VMEM, pltpu.SemaphoreType.DMA
    return pl.pallas_call(
        functools.partial(kernel, n_tgt, n_hist, norm),
        out_shape=jax.ShapeDtypeStruct((STEPS, 2, tt, band, n), F32),
        in_specs=[pl.BlockSpec(memory_space=pl.ANY)] * 4,
        out_specs=pl.BlockSpec(memory_space=pltpu.VMEM),
        scratch_shapes=[
            vmem((tt, 2, sh, n, n), F32),
            vmem((tt, 3 * sh * n, 2 * n), BF16),
            vmem((2 * n, 3 * sh * n), BF16),
            vmem((tt, 2 * n, 2 * n), F32),
            vmem((STEPS, 2, sh, n, n), F32),
            vmem((2, tt, n, n), F32),
            vmem((2, n, n), F32),
            vmem((last, hp, sh, 2, n, n), F32),
            vmem((last, hp, sh, 2, n, n), F32),
            vmem((last, sh, 2, n, n), F32),
            vmem((last, sh, 2, n, n), F32),
            vmem((last, sh, 2, n, n), F32),
            vmem((last, 2, sh, n, n), F32),
            vmem((STEPS, sh, 3 * n, 2 * n), BF16),
            vmem((sh, 2, n, n), F32),
            vmem((STEPS, STEPS, 2, n, n), F32),
            vmem((STEPS, 2 * n, 3 * n), BF16),
            vmem((last, 2, tt, band, n), F32),
            vmem((n_cut, nz, hp, su, 2, band, n), F32),
            vmem((n_cut, hp, nz, su, 2, band, n), F32),
            vmem((n_cut, nz, su, 2, band, n), F32),
            vmem((n_cut, nz, su, 2, band, n), F32),
            vmem((n_cut, nz, su, 2, band, n), F32),
            sem((tt,)),
            sem((3,)),
            sem((last, hp, sh)),
            sem((last, hp, sh)),
            sem((last, sh, PIECES)),
            sem((last, sh, PIECES)),
            sem((last, sh, PIECES)),
            sem((STEPS, 2, PIECES, sh)),
            sem((STEPS, PIECES, sh)),
            sem((STEPS, STEPS)),
            sem((STEPS, STEPS, hp)),
            sem((STEPS, STEPS)),
            sem((last, n_hist)),
            sem((last, hp)),
            sem((n_cut, hp)),
            sem((n_cut, hp)),
            sem((n_cut, nz)),
            sem((n_cut, nz)),
            sem((n_cut, nz)),
        ],
        compiler_params=pltpu.CompilerParams(
            collective_id=0, has_side_effects=True, vmem_limit_bytes=56 * 2**20
        ),
    )(history, self_energy, green_row, propagator)


def solution(mesh):
    in_specs = (
        P(None, "hist", "tgt", None, None),
        P(None, "hist", None, None),
        P(None, "tgt", None, None),
        P(),
    )
    out_specs = P(None, None, "tgt", "hist", None)
    return jax.shard_map(
        per_device, mesh=mesh, in_specs=in_specs, out_specs=out_specs, check_vma=False
    )
```

```python
import functools

import jax
import jax.numpy as jnp
from jax import lax
from jax.experimental import pallas as pl
from jax.experimental.pallas import tpu as pltpu
from jax.sharding import PartitionSpec as P

STEPS = 4
COUPLING = 1.5
MIXING = 0.7
MESH = pl.DeviceIdType.MESH
CUTS = 2
PIECES = 4
F32, BF16 = jnp.float32, jnp.bfloat16


def split(value):
    high = value.astype(BF16)
    return high, (value - high.astype(F32)).astype(BF16)


def complex_of(product):
    n = product.shape[0] // 2
    return product[:n, :n] - product[n:, n:], product[:n, n:] + product[n:, :n]


def snake(index):
    q, r = index // 2, index % 2
    return 2 * q + r + (q % 2) * (1 - 2 * r)


def kernel(
    n_tgt, n_hist, norm,
    h_hbm, s_hbm, r_hbm, p_hbm, out_ref,
    hst, h3, s3, acc, sbuf, total, rin, pin, exs, exr, own, upb, dnb, rows, x3, base, sxb, l3, outb,
    fin, exf, fsum, upf, dnf,
    h_sem, in_sem, ex_s, ex_r, ch_s, up_r, dn_r, rg_s, rg_r, sx_s, sy_s, sx_r, bd_s, bd_r,
    fx_s, fx_r, fc_s, fu_r, fd_r,
):
    _, sh, tt_all, n, _ = h_hbm.shape
    hp = n_hist // n_tgt
    nz = n_hist // hp
    band = n // n_hist
    depth = sh * n
    g, h = lax.axis_index("tgt"), lax.axis_index("hist")
    z, c = h // hp, h % hp
    root = z == g
    pos = snake(g)
    rel = (pos - snake(z) + n_tgt) % n_tgt
    ahead, behind = snake((pos + 1) % n_tgt), snake((pos + n_tgt - 1) % n_tgt)
    last = STEPS - 1

    def remote(src, dst, send_sem, recv_sem, tgt, hist):
        return pltpu.make_async_remote_copy(
            src_ref=src, dst_ref=dst, send_sem=send_sem, recv_sem=recv_sem,
            device_id={"tgt": tgt, "hist": hist}, device_id_type=MESH,
        )

    def loop(count, body):
        lax.fori_loop(0, count, lambda i, _: (body(i), None)[1], None)

    def turn(i):
        tt, d = i // hp, (i % hp + 1) % hp
        return tt, d, (c + d) % hp * sh + tt

    def h_copy(t):
        return pltpu.make_async_copy(h_hbm.at[:, :, t], hst.at[t], h_sem.at[t])

    s_copy = pltpu.make_async_copy(s_hbm, sbuf.at[0], in_sem.at[0])
    p_copy = pltpu.make_async_copy(p_hbm, pin, in_sem.at[1])
    r_copy = pltpu.make_async_copy(r_hbm, rin, in_sem.at[2])
    s_copy.start()
    loop(tt_all, lambda i: h_copy(turn(i)[2]).start())
    p_copy.start()
    r_copy.start()

    barrier = pltpu.get_barrier_semaphore()
    for e in range(1, n_hist):
        pl.semaphore_signal(
            barrier, inc=1, device_id={"tgt": g, "hist": (h + e) % n_hist}, device_id_type=MESH
        )
    for near in (ahead, behind):
        pl.semaphore_signal(barrier, inc=1, device_id={"tgt": near, "hist": h}, device_id_type=MESH)

    def store_x3(slot, tt, real, imag):
        for at, value in ((0, real), (n, imag)):
            high, low = split(value)
            cols = pl.ds(at, n)
            x3[slot, tt, pl.ds(0, n), cols] = high
            x3[slot, tt, pl.ds(n, n), cols] = low
            x3[slot, tt, pl.ds(2 * n, n), cols] = high

    def store_l3(slot, real, imag):
        for at, value in ((0, real), (n, imag)):
            high, low = split(value)
            l3[slot, pl.ds(at, n), pl.ds(0, n)] = high
            l3[slot, pl.ds(at, n), pl.ds(n, n)] = high
            l3[slot, pl.ds(at, n), pl.ds(2 * n, n)] = low

    half = sh // 2
    width = 3 * n

    def store_s3(step, s):
        for part in range(2):
            high, low = split(sbuf[step, part, s])
            r = pl.ds(part * n, n)
            s3[r, pl.ds(s * width, n)] = high
            s3[r, pl.ds(s * width + n, n)] = high
            s3[r, pl.ds(s * width + 2 * n, n)] = low
        if s == 0:

            @pl.when(h < step)
            def _():
                s3[:, pl.ds(0, width)] = jnp.zeros((2 * n, width), BF16)

    def store_h3(t):
        h_copy(t).wait()
        for s in range(sh):
            for part in range(2):
                high, low = split(hst[t, part, s])
                cols = pl.ds(part * n, n)
                h3[t, pl.ds(s * width, n), cols] = high
                h3[t, pl.ds(s * width + n, n), cols] = low
                h3[t, pl.ds(s * width + 2 * n, n), cols] = high

    def dot_of(t, begin, end):
        at = pl.ds(begin * width, (end - begin) * width)
        return jnp.dot(s3[:, at], h3[t, at, :], preferred_element_type=F32)

    def term(t):
        real, imag = complex_of(acc[t] + dot_of(t, half, sh))
        return (MIXING * norm) * imag, (-MIXING * norm) * real

    def ex_copy(step, d, tt):
        return remote(
            exs.at[step, d, tt], exr.at[step, d, tt], ex_s.at[step, d, tt], ex_r.at[step, d, tt],
            g, z * hp + (c + d) % hp,
        )

    def piece(p):
        return pl.ds(p * (n // PIECES), n // PIECES)

    def chain_copy(step, tt, p, up):
        at = piece(p)
        return remote(
            own.at[step, tt, :, at], (upb if up else dnb).at[step, tt, :, at],
            ch_s.at[step, tt, p], (up_r if up else dn_r).at[step, tt, p],
            g, h + hp if up else h - hp,
        )

    def ring_copy(step, p, s, way):
        ref = sbuf.at[step, :, s, piece(p)]
        return remote(
            ref, ref, rg_s.at[step, way, p, s], rg_r.at[step, p, s],
            behind if way else ahead, h,
        )

    reach = (n_tgt // 2, n_tgt // 2 - 1)
    ring_gives = [(rel < reach[p], (rel == 0) | (rel >= reach[p] + 2)) for p in range(2)] * (PIECES // 2)

    def ring_give(step, s, p):
        for way in (p % 2, 1 - p % 2):

            @pl.when(ring_gives[p][way])
            def _():
                ring_copy(step, p, s, way).start()

    def sx_copy(step, k):
        return remote(
            sbuf.at[step, :, 0], sxb.at[step, k], sx_s.at[step, k], sx_r.at[step, k],
            g, g * hp + k % hp,
        )

    def sy_copy(step, k, d):
        return remote(
            sxb.at[step, k], sxb.at[step, k], sy_s.at[step, k, d], sx_r.at[step, k],
            g, z * hp + (c + d) % hp,
        )

    def band_copy(step, e, sender):
        to = (h + e) % n_hist
        return remote(
            rows.at[step, :, :, pl.ds(pl.multiple_of(to * band, band), band)],
            outb.at[step, :, pl.ds(sender * sh, sh)], bd_s.at[step, e], bd_r.at[step, sender],
            g, to,
        )

    def fin_ex_copy(q, d):
        to = (c + d) % hp
        return remote(
            fin.at[q, :, to], exf.at[q, d], fx_s.at[q, d], fx_r.at[q, d], g, z * hp + to
        )

    def fin_chain_copy(q, zz, up):
        return remote(
            fsum.at[q, zz], (upf if up else dnf).at[q, zz], fc_s.at[q, zz],
            (fu_r if up else fd_r).at[q, zz], g, h + hp if up else h - hp,
        )

    def receive_s(step, s):
        @pl.when((rel > 0) & (step > 0))
        def _():
            for p in range(PIECES):
                ring_copy(step, p, s, 0).wait_recv()
                ring_give(step, s, p)

        if s == 0:

            @pl.when((h < step) & root)
            def _():
                sxb[step, h] = sbuf[step, :, 0]

            @pl.when((h < step) & (z != g))
            def _():
                sx_copy(step, h).start()

    def make_base(step):
        def slot(k):
            @pl.when(h != k)
            def _():
                sx_copy(step, k).wait_recv()

            @pl.when(c == k % hp)
            def _():
                for d in range(1, hp):
                    sy_copy(step, k, d).start()

            store_l3(k + 1, norm * sxb[step, k, 1], -norm * sxb[step, k, 0])

        loop(step, slot)

        def one(tt):
            total[...] = jnp.dot(l3[0], x3[step, tt], preferred_element_type=F32)

            def add(k):
                total[...] += jnp.dot(l3[k + 1], x3[k + 1, tt], preferred_element_type=F32)

            loop(step, add)
            real, imag = complex_of(total[...])
            base[tt, 0] = MIXING * real
            base[tt, 1] = MIXING * imag

        loop(sh, one)

    def sent(step):
        for p in range(PIECES):
            for way in range(2):

                @pl.when(ring_gives[p][way])
                def _():
                    loop(sh, lambda s: ring_copy(step, p, s, way).wait_send())

        @pl.when((h < step) & (z != g))
        def _():
            sx_copy(step, h).wait_send()

        @pl.when(root)
        def _():
            def slot(k):
                @pl.when(c == k % hp)
                def _():
                    for d in range(1, hp):
                        sy_copy(step, k, d).wait_send()

            loop(step, slot)

    def sums_sent(step):
        for d in range(1, hp):
            loop(sh, lambda tt: ex_copy(step, d, tt).wait_send())
        for up, gives in ((True, z < g), (False, z > g)):

            @pl.when(gives)
            def _():
                for p in range(PIECES):
                    loop(sh, lambda tt: chain_copy(step, tt, p, up).wait_send())

    def bands_sent(step):
        @pl.when(root)
        def _():
            loop(n_hist - 1, lambda e: band_copy(step, e + 1, c).wait_send())

    n_cut, su = fin.shape[0], fin.shape[3]
    per_core = n_cut // hp

    def first_link(step, tt):
        for d in range(1, hp):
            ex_copy(step, d, tt).wait_recv()
            own[step, tt] += exr[step, d, tt]

        @pl.when((z < g) & (z == 0))
        def _():
            for p in range(PIECES):
                chain_copy(step, tt, p, True).start()

        @pl.when((z > g) & (z == nz - 1))
        def _():
            for p in range(PIECES):
                chain_copy(step, tt, p, False).start()

    def link(step, tt):
        for p in range(PIECES):
            at = piece(p)

            @pl.when((z > 0) & (z <= g))
            def _():
                chain_copy(step, tt, p, True).wait_recv()
                own[step, tt, :, at] += upb[step, tt, :, at]

            @pl.when((z < nz - 1) & (z >= g))
            def _():
                chain_copy(step, tt, p, False).wait_recv()
                own[step, tt, :, at] += dnb[step, tt, :, at]

            @pl.when((z < g) & (z > 0))
            def _():
                chain_copy(step, tt, p, True).start()

            @pl.when((z > g) & (z < nz - 1))
            def _():
                chain_copy(step, tt, p, False).start()

            @pl.when(root)
            def _():
                real = own[step, tt, 0, at] + base[tt, 0, at]
                imag = own[step, tt, 1, at] + base[tt, 1, at]
                modulus = real * real + imag * imag
                factor = -COUPLING * modulus / (1.0 + modulus)
                sbuf[step + 1, 0, tt, at] = factor * real
                sbuf[step + 1, 1, tt, at] = factor * imag
                ring_give(step + 1, tt, p)
                rows[step, 0, tt, at] = real
                rows[step, 1, tt, at] = imag

        @pl.when(root)
        def _():
            store_x3(step + 1, tt, rows[step, 0, tt], rows[step, 1, tt])

    def far(u, go):
        for dist in range(nz - 1, 0, -1):
            for up in (True, False):
                zz = z + dist if up else z - dist
                on_way = zz < nz if up else zz >= 0
                go(u, zz, up, on_way, z == 0 if up else z == nz - 1)

    def far_first(u, zz, up, on_way, first):
        @pl.when(on_way & first)
        def _():
            fin_chain_copy(u, zz, up).start()

    def far_next(u, zz, up, on_way, first):
        @pl.when(on_way & jnp.logical_not(first))
        def _():
            fin_chain_copy(u, zz, up).wait_recv()
            fsum[u, zz] += (upf if up else dnf)[u, zz]
            fin_chain_copy(u, zz, up).start()

    def far_sent(u, zz, up, on_way, first):
        @pl.when(on_way)
        def _():
            fin_chain_copy(u, zz, up).wait_send()

    def of_pair(u):
        for d in range(1, hp):
            fin_ex_copy(u, d).wait_recv()
        for zz in range(nz):
            value = fin[u, zz, c]
            for d in range(1, hp):
                value += exf[u, d, zz]
            fsum[u, zz] = value
        far(u, far_first)

    def product(step, i):
        tt, d, t = turn(i)
        is_last = step // last
        t = is_last * i + (1 - is_last) * t

        @pl.when(step == 0)
        def _():
            store_h3(t)
            acc[t] = dot_of(t, 0, half)

        real, imag = term(t)

        @pl.when((step < last) & (d > 0))
        def _():
            exs[step, d, tt, 0], exs[step, d, tt, 1] = real, imag
            ex_copy(step, d, tt).start()

        @pl.when((step < last) & (d == 0))
        def _():
            own[step, tt, 0], own[step, tt, 1] = real, imag
            pl.when(tt > 0)(lambda: first_link(step, tt - 1))

        @pl.when(step == last)
        def _():
            u, r = i // su, i % su
            for part, value in enumerate((real, imag)):
                for b in range(n_hist):
                    fin[u, b // hp, b % hp, r, part] = value[b * band : (b + 1) * band]

            @pl.when(root & (c == u // per_core))
            def _():
                for part in range(2):
                    for b in range(n_hist):
                        fin[u, b // hp, b % hp, r, part] += base[
                            u % per_core * su + r, part, pl.ds(b * band, band)
                        ]

            @pl.when(r == su - 1)
            def _():
                for d in range(1, hp):
                    fin_ex_copy(u, d).start()
                pl.when(u > 0)(lambda: of_pair(u - 1))

    def run(step):
        @pl.when(step > 0)
        def _():
            sums_sent(step - 1)

        @pl.when(step > 1)
        def _():
            sent(step - 1)
            bands_sent(step - 2)

        for s in range(half):
            receive_s(step, s)
            store_s3(step, s)

        @pl.when(step > 0)
        def _():
            def one(t):
                acc[t] = dot_of(t, 0, half)

            loop(tt_all, one)

        for s in range(half, sh):
            receive_s(step, s)
            store_s3(step, s)
        pl.when(root)(lambda: make_base(step))
        loop(tt_all, lambda i: product(step, i))

        @pl.when(step < last)
        def _():
            first_link(step, sh - 1)
            loop(sh, lambda tt: link(step, tt))

            @pl.when(root)
            def _():
                outb[step, :, pl.ds(c * sh, sh)] = rows[
                    step, :, :, pl.ds(pl.multiple_of(h * band, band), band)
                ]
                loop(n_hist - 1, lambda e: band_copy(step, e + 1, c).start())

    s_copy.wait()
    p_copy.wait()
    r_copy.wait()

    @pl.when(root)
    def _():
        store_l3(0, pin[0], pin[1])
        loop(sh, lambda tt: store_x3(0, tt, rin[0, c * sh + tt], rin[1, c * sh + tt]))

    pl.semaphore_wait(barrier, n_hist + 1)
    loop(STEPS, run)

    of_pair(n_cut - 1)
    loop(n_cut, lambda u: far(u, far_next))
    for step in range(last):
        for sender in range(hp):

            @pl.when(h != g * hp + sender)
            def _():
                band_copy(step, 1, sender).wait_recv()

        out_ref[step] = outb[step]
    sent(last)
    bands_sent(last - 1)

    def finish(u):
        @pl.when(z > 0)
        def _():
            fin_chain_copy(u, z, True).wait_recv()
            fsum[u, z] += upf[u, z]

        @pl.when(z < nz - 1)
        def _():
            fin_chain_copy(u, z, False).wait_recv()
            fsum[u, z] += dnf[u, z]

        for i in range(su):
            for part in range(2):
                out_ref[last, part, u * su + i] = fsum[u, z, i, part]

    loop(n_cut, finish)

    def finish_sent(u):
        for d in range(1, hp):
            fin_ex_copy(u, d).wait_send()
        far(u, far_sent)

    loop(n_cut, finish_sent)


def per_device(history, self_energy, green_row, propagator):
    n_tgt, n_hist = lax.axis_size("tgt"), lax.axis_size("hist")
    _, sh, tt, n, _ = history.shape
    hp, band, last = n_hist // n_tgt, n // n_hist, STEPS - 1
    nz = n_hist // hp
    norm = float(sh * n_hist * n) ** (-0.5)
    n_cut = hp * CUTS
    su = tt // n_cut
    vmem, sem = pltpu.VMEM, pltpu.SemaphoreType.DMA
    return pl.pallas_call(
        functools.partial(kernel, n_tgt, n_hist, norm),
        out_shape=jax.ShapeDtypeStruct((STEPS, 2, tt, band, n), F32),
        in_specs=[pl.BlockSpec(memory_space=pl.ANY)] * 4,
        out_specs=pl.BlockSpec(memory_space=pltpu.VMEM),
        scratch_shapes=[
            vmem((tt, 2, sh, n, n), F32),
            vmem((tt, 3 * sh * n, 2 * n), BF16),
            vmem((2 * n, 3 * sh * n), BF16),
            vmem((tt, 2 * n, 2 * n), F32),
            vmem((STEPS, 2, sh, n, n), F32),
            vmem((2 * n, 2 * n), F32),
            vmem((2, tt, n, n), F32),
            vmem((2, n, n), F32),
            vmem((last, hp, sh, 2, n, n), F32),
            vmem((last, hp, sh, 2, n, n), F32),
            vmem((last, sh, 2, n, n), F32),
            vmem((last, sh, 2, n, n), F32),
            vmem((last, sh, 2, n, n), F32),
            vmem((last, 2, sh, n, n), F32),
            vmem((STEPS, sh, 3 * n, 2 * n), BF16),
            vmem((sh, 2, n, n), F32),
            vmem((STEPS, STEPS, 2, n, n), F32),
            vmem((STEPS, 2 * n, 3 * n), BF16),
            vmem((last, 2, tt, band, n), F32),
            vmem((n_cut, nz, hp, su, 2, band, n), F32),
            vmem((n_cut, hp, nz, su, 2, band, n), F32),
            vmem((n_cut, nz, su, 2, band, n), F32),
            vmem((n_cut, nz, su, 2, band, n), F32),
            vmem((n_cut, nz, su, 2, band, n), F32),
            sem((tt,)),
            sem((3,)),
            sem((last, hp, sh)),
            sem((last, hp, sh)),
            sem((last, sh, PIECES)),
            sem((last, sh, PIECES)),
            sem((last, sh, PIECES)),
            sem((STEPS, 2, PIECES, sh)),
            sem((STEPS, PIECES, sh)),
            sem((STEPS, STEPS)),
            sem((STEPS, STEPS, hp)),
            sem((STEPS, STEPS)),
            sem((last, n_hist)),
            sem((last, hp)),
            sem((n_cut, hp)),
            sem((n_cut, hp)),
            sem((n_cut, nz)),
            sem((n_cut, nz)),
            sem((n_cut, nz)),
        ],
        compiler_params=pltpu.CompilerParams(
            collective_id=0, has_side_effects=True, vmem_limit_bytes=56 * 2**20
        ),
    )(history, self_energy, green_row, propagator)


def solution(mesh):
    in_specs = (
        P(None, "hist", "tgt", None, None),
        P(None, "hist", None, None),
        P(None, "tgt", None, None),
        P(),
    )
    out_specs = P(None, None, "tgt", "hist", None)
    return jax.shard_map(
        per_device, mesh=mesh, in_specs=in_specs, out_specs=out_specs, check_vma=False
    )
```

```python
import functools

import jax
import jax.numpy as jnp
from jax import lax
from jax.experimental import pallas as pl
from jax.experimental.pallas import tpu as pltpu
from jax.sharding import PartitionSpec as P

STEPS = 4
COUPLING = 1.5
MIXING = 0.7
MESH = pl.DeviceIdType.MESH
CUTS = 2
PIECES = 4
F32, BF16 = jnp.float32, jnp.bfloat16


def split(value):
    high = value.astype(BF16)
    return high, (value - high.astype(F32)).astype(BF16)


def complex_of(product):
    n = product.shape[0] // 2
    return product[:n, :n] - product[n:, n:], product[:n, n:] + product[n:, :n]


def snake(index):
    q, r = index // 2, index % 2
    return 2 * q + r + (q % 2) * (1 - 2 * r)


def kernel(
    n_tgt, n_hist, norm,
    h_hbm, s_hbm, r_hbm, p_hbm, out_ref,
    hst, h3, s3, acc, sbuf, rin, pin, exs, exr, own, upb, dnb, rows, x3, base, sxb, l3, outb,
    fin, exf, fsum, upf, dnf,
    h_sem, in_sem, ex_s, ex_r, ch_s, up_r, dn_r, rg_s, rg_r, sx_s, sy_s, sx_r, bd_s, bd_r,
    fx_s, fx_r, fc_s, fu_r, fd_r,
):
    _, sh, tt_all, n, _ = h_hbm.shape
    hp = n_hist // n_tgt
    nz = n_hist // hp
    band = n // n_hist
    depth = sh * n
    g, h = lax.axis_index("tgt"), lax.axis_index("hist")
    z, c = h // hp, h % hp
    root = z == g
    middle = (z != g) & (z > 0) & (z < nz - 1)
    pos = snake(g)
    rel = (pos - snake(z) + n_tgt) % n_tgt
    ahead, behind = snake((pos + 1) % n_tgt), snake((pos + n_tgt - 1) % n_tgt)
    last = STEPS - 1
    sends, bands_sent, older = [], [], []

    def remote(src, dst, send_sem, recv_sem, tgt, hist):
        return pltpu.make_async_remote_copy(
            src_ref=src, dst_ref=dst, send_sem=send_sem, recv_sem=recv_sem,
            device_id={"tgt": tgt, "hist": hist}, device_id_type=MESH,
        )

    def loop(count, body):
        lax.fori_loop(0, count, lambda i, _: (body(i), None)[1], None)

    def h_copy(t):
        return pltpu.make_async_copy(h_hbm.at[:, :, t], hst.at[t], h_sem.at[t])

    s_copy = pltpu.make_async_copy(s_hbm, sbuf.at[0], in_sem.at[0])
    p_copy = pltpu.make_async_copy(p_hbm, pin, in_sem.at[1])
    r_copy = pltpu.make_async_copy(r_hbm, rin, in_sem.at[2])
    s_copy.start()
    loop(tt_all, lambda i: h_copy((c + i % hp + 1) % hp * sh + i // hp).start())
    p_copy.start()
    r_copy.start()

    barrier = pltpu.get_barrier_semaphore()
    for e in range(1, n_hist):
        pl.semaphore_signal(
            barrier, inc=1, device_id={"tgt": g, "hist": (h + e) % n_hist}, device_id_type=MESH
        )
    for near in (ahead, behind):
        pl.semaphore_signal(barrier, inc=1, device_id={"tgt": near, "hist": h}, device_id_type=MESH)

    def store_x3(slot, tt, real, imag):
        for at, value in ((0, real), (n, imag)):
            high, low = split(value)
            cols = pl.ds(at, n)
            x3[slot, tt, pl.ds(0, n), cols] = high
            x3[slot, tt, pl.ds(n, n), cols] = low
            x3[slot, tt, pl.ds(2 * n, n), cols] = high

    def store_l3(slot, real, imag):
        for at, value in ((0, real), (n, imag)):
            high, low = split(value)
            l3[slot, pl.ds(at, n), pl.ds(0, n)] = high
            l3[slot, pl.ds(at, n), pl.ds(n, n)] = high
            l3[slot, pl.ds(at, n), pl.ds(2 * n, n)] = low

    half = sh // 2
    width = 3 * n

    def store_s3(step, s):
        for part in range(2):
            high, low = split(sbuf[step, part, s])
            r = pl.ds(part * n, n)
            s3[r, pl.ds(s * width, n)] = high
            s3[r, pl.ds(s * width + n, n)] = high
            s3[r, pl.ds(s * width + 2 * n, n)] = low
        if step > 0 and s == 0:

            @pl.when(h < step)
            def _():
                s3[:, pl.ds(0, width)] = jnp.zeros((2 * n, width), BF16)

    def store_h3(t):
        h_copy(t).wait()
        for s in range(sh):
            for part in range(2):
                high, low = split(hst[t, part, s])
                cols = pl.ds(part * n, n)
                h3[t, pl.ds(s * width, n), cols] = high
                h3[t, pl.ds(s * width + n, n), cols] = low
                h3[t, pl.ds(s * width + 2 * n, n), cols] = high

    def dot_of(t, begin, end):
        at = pl.ds(begin * width, (end - begin) * width)
        return jnp.dot(s3[:, at], h3[t, at, :], preferred_element_type=F32)

    def term(t, step):
        if step == 0:
            store_h3(t)
            product = dot_of(t, 0, sh)
        else:
            product = acc[t] + dot_of(t, half, sh)
        real, imag = complex_of(product)
        return (MIXING * norm) * imag, (-MIXING * norm) * real

    def ex_copy(step, d, tt):
        return remote(
            exs.at[step, d, tt], exr.at[step, d, tt], ex_s.at[step, d, tt], ex_r.at[step, d, tt],
            g, z * hp + (c + d) % hp,
        )

    def piece(p):
        return pl.ds(p * (n // PIECES), n // PIECES)

    def chain_copy(step, tt, p, up):
        at = piece(p)
        return remote(
            own.at[step, tt, :, at], (upb if up else dnb).at[step, tt, :, at],
            ch_s.at[step, tt, p], (up_r if up else dn_r).at[step, tt, p],
            g, h + hp if up else h - hp,
        )

    def ring_copy(step, p, s, way):
        ref = sbuf.at[step, :, s, piece(p)]
        return remote(
            ref, ref, rg_s.at[step, way, p, s], rg_r.at[step, p, s],
            behind if way else ahead, h,
        )

    reach = (n_tgt // 2, n_tgt // 2 - 1)
    ring_gives = [(rel < reach[p], (rel == 0) | (rel >= reach[p] + 2)) for p in range(2)] * (PIECES // 2)

    def ring_give(step, s, p):
        for way in (p % 2, 1 - p % 2):

            @pl.when(ring_gives[p][way])
            def _():
                ring_copy(step, p, s, way).start()

    def sx_copy(step, k):
        return remote(
            sbuf.at[step, :, 0], sxb.at[step, k], sx_s.at[step, k], sx_r.at[step, k],
            g, g * hp + k % hp,
        )

    def sy_copy(step, k, d):
        return remote(
            sxb.at[step, k], sxb.at[step, k], sy_s.at[step, k, d], sx_r.at[step, k],
            g, z * hp + (c + d) % hp,
        )

    def band_copy(step, e, sender):
        to = (h + e) % n_hist
        return remote(
            rows.at[step, :, :, pl.ds(pl.multiple_of(to * band, band), band)],
            outb.at[step, :, pl.ds(sender * sh, sh)], bd_s.at[step, e], bd_r.at[step, sender],
            g, to,
        )

    def fin_ex_copy(q, d):
        to = (c + d) % hp
        return remote(
            fin.at[q, :, to], exf.at[q, d], fx_s.at[q, d], fx_r.at[q, d], g, z * hp + to
        )

    def fin_chain_copy(q, zz, up):
        return remote(
            fsum.at[q, zz], (upf if up else dnf).at[q, zz], fc_s.at[q, zz],
            (fu_r if up else fd_r).at[q, zz], g, h + hp if up else h - hp,
        )

    def receive_s(step, s):
        @pl.when(rel > 0)
        def _():
            for p in range(PIECES):
                ring_copy(step, p, s, 0).wait_recv()
                ring_give(step, s, p)

        for p in range(PIECES):
            for way in range(2):
                sends.append(
                    (ring_gives[p][way], lambda p=p, way=way: ring_copy(step, p, s, way).wait_send())
                )
        if s > 0:
            return
        for k in range(min(step, n_hist)):

            @pl.when((h == k) & root)
            def _():
                sxb[step, k] = sbuf[step, :, 0]

            away = (h == k) & (z != g)

            @pl.when(away)
            def _():
                sx_copy(step, k).start()

            sends.append((away, lambda k=k: sx_copy(step, k).wait_send()))

    def first_sums(step):
        for s in range(half):
            receive_s(step, s)
            store_s3(step, s)

        def one(i):
            pair = [dot_of(2 * i + j, 0, half) for j in range(2)]
            for j in range(2):
                acc[2 * i + j] = pair[j]

        loop(tt_all // 2, one)
        for s in range(half, sh):
            receive_s(step, s)
            store_s3(step, s)

    def flush(waits):
        for gives, wait in waits:
            if gives is None:
                wait()
            else:
                pl.when(gives)(wait)
        waits.clear()

    def make_base(step):
        for k in range(min(step, n_hist)):

            @pl.when(h != k)
            def _():
                sx_copy(step, k).wait_recv()

            @pl.when(c == k % hp)
            def _():
                for d in range(1, hp):
                    sy_copy(step, k, d).start()

            store_l3(k + 1, norm * sxb[step, k, 1], -norm * sxb[step, k, 0])

        def one(tt):
            total = jnp.dot(l3[0], x3[step, tt], preferred_element_type=F32)
            for k in range(min(step, n_hist)):
                total += jnp.dot(l3[k + 1], x3[k + 1, tt], preferred_element_type=F32)
            real, imag = complex_of(total)
            base[tt, 0] = MIXING * real
            base[tt, 1] = MIXING * imag

        loop(sh, one)

    s_copy.wait()
    for s in range(sh):
        store_s3(0, s)
    pl.semaphore_wait(barrier, n_hist + 1)

    for step in range(last):
        if step > 0:
            flush(sends)
            flush(older)
            older, bands_sent = bands_sent, []
            first_sums(step)

        def first_link(tt, step=step):
            for d in range(1, hp):
                ex_copy(step, d, tt).wait_recv()
                own[step, tt] += exr[step, d, tt]

            @pl.when((z < g) & (z == 0))
            def _():
                for p in range(PIECES):
                    chain_copy(step, tt, p, True).start()

            @pl.when((z > g) & (z == nz - 1))
            def _():
                for p in range(PIECES):
                    chain_copy(step, tt, p, False).start()

        def relay(tt, step=step):
            for up, here in ((True, z < g), (False, z > g)):

                @pl.when(here)
                def _():
                    for p in range(PIECES):
                        at = piece(p)
                        chain_copy(step, tt, p, up).wait_recv()
                        own[step, tt, :, at] += (upb if up else dnb)[step, tt, :, at]
                        chain_copy(step, tt, p, up).start()

        def products(tt, step=step):
            terms = [term((c + d) % hp * sh + tt, step) for d in [*range(1, hp), 0]]
            for d in range(1, hp):
                exs[step, d, tt, 0], exs[step, d, tt, 1] = terms[d - 1]
                ex_copy(step, d, tt).start()
            own[step, tt, 0], own[step, tt, 1] = terms[hp - 1]
            pl.when(tt > 0)(lambda: first_link(tt - 1))
            pl.when(middle & (tt > 1))(lambda: relay(tt - 2))

        loop(sh, products)
        first_link(sh - 1)
        pl.when(middle)(lambda: loop(2, lambda i: relay(sh - 2 + i)))
        for d in range(1, hp):
            sends.append((None, lambda d=d, step=step: loop(sh, lambda tt: ex_copy(step, d, tt).wait_send())))
        if step == 0:
            p_copy.wait()
            r_copy.wait()

        @pl.when(root)
        def _():
            if step == 0:
                store_l3(0, pin[0], pin[1])
                loop(sh, lambda tt: store_x3(0, tt, rin[0, c * sh + tt], rin[1, c * sh + tt]))
            make_base(step)

        def link(tt):
            for p in range(PIECES):
                at = piece(p)

                @pl.when(z > 0)
                def _():
                    chain_copy(step, tt, p, True).wait_recv()
                    own[step, tt, :, at] += upb[step, tt, :, at]

                @pl.when(z < nz - 1)
                def _():
                    chain_copy(step, tt, p, False).wait_recv()
                    own[step, tt, :, at] += dnb[step, tt, :, at]

                real = own[step, tt, 0, at] + base[tt, 0, at]
                imag = own[step, tt, 1, at] + base[tt, 1, at]
                modulus = real * real + imag * imag
                factor = -COUPLING * modulus / (1.0 + modulus)
                sbuf[step + 1, 0, tt, at] = factor * real
                sbuf[step + 1, 1, tt, at] = factor * imag
                ring_give(step + 1, tt, p)
                rows[step, 0, tt, at] = real
                rows[step, 1, tt, at] = imag
            store_x3(step + 1, tt, rows[step, 0, tt], rows[step, 1, tt])

        pl.when(root)(lambda: loop(sh, link))
        for up, gives in ((True, z < g), (False, z > g)):
            for p in range(PIECES):
                sends.append(
                    (gives, lambda p=p, up=up, step=step: loop(sh, lambda tt: chain_copy(step, tt, p, up).wait_send()))
                )
        for k in range(min(step, n_hist)):
            for d in range(1, hp):
                sends.append((root & (c == k % hp), lambda k=k, d=d, step=step: sy_copy(step, k, d).wait_send()))

        @pl.when(root)
        def _():
            outb[step, :, pl.ds(c * sh, sh)] = rows[
                step, :, :, pl.ds(pl.multiple_of(h * band, band), band)
            ]
            loop(n_hist - 1, lambda e: band_copy(step, e + 1, c).start())

        bands_sent.append(
            (root, lambda step=step: loop(n_hist - 1, lambda e: band_copy(step, e + 1, c).wait_send()))
        )

    flush(sends)
    flush(older)
    first_sums(last)
    for k in range(min(last, n_hist)):
        for d in range(1, hp):
            sends.append((root & (c == k % hp), lambda k=k, d=d: sy_copy(last, k, d).wait_send()))
    pl.when(root)(lambda: make_base(last))
    n_cut, su = fin.shape[0], fin.shape[3]
    per_core = n_cut // hp

    def far(u, go):
        for dist in range(nz - 1, 0, -1):
            for up in (True, False):
                zz = z + dist if up else z - dist
                on_way = zz < nz if up else zz >= 0
                go(u, zz, up, on_way, z == 0 if up else z == nz - 1)

    def far_first(u, zz, up, on_way, first):
        @pl.when(on_way & first)
        def _():
            fin_chain_copy(u, zz, up).start()

    def far_next(u, zz, up, on_way, first):
        @pl.when(on_way & jnp.logical_not(first))
        def _():
            fin_chain_copy(u, zz, up).wait_recv()
            fsum[u, zz] += (upf if up else dnf)[u, zz]
            fin_chain_copy(u, zz, up).start()

        sends.append((on_way, lambda: fin_chain_copy(u, zz, up).wait_send()))

    def of_pair(u):
        for d in range(1, hp):
            fin_ex_copy(u, d).wait_recv()

        def both(zz):
            value = fin[u, zz, c]
            for d in range(1, hp):
                value += exf[u, d, zz]
            fsum[u, zz] = value

        loop(nz, both)
        far(u, far_first)

    for u in range(n_cut):

        def bands(i, u=u):
            for part, value in enumerate(term(u * su + i, last)):
                for b in range(n_hist):
                    fin[u, b // hp, b % hp, i, part] = value[b * band : (b + 1) * band]

        loop(su, bands)

        @pl.when(root & (c == u // per_core))
        def _():
            def add(i):
                for part in range(2):
                    for b in range(n_hist):
                        fin[u, b // hp, b % hp, i, part] += base[
                            u % per_core * su + i, part, pl.ds(b * band, band)
                        ]

            loop(su, add)

        for d in range(1, hp):
            fin_ex_copy(u, d).start()
            sends.append((None, lambda u=u, d=d: fin_ex_copy(u, d).wait_send()))
        if u > 0:
            of_pair(u - 1)
        if u > 1:
            far(u - 2, far_next)
    of_pair(n_cut - 1)
    for u in range(max(0, n_cut - 2), n_cut):
        far(u, far_next)
    for step in range(last):
        for sender in range(hp):

            @pl.when(h != g * hp + sender)
            def _():
                band_copy(step, 1, sender).wait_recv()

        out_ref[step] = outb[step]
    for u in range(n_cut):

        @pl.when(z > 0)
        def _():
            fin_chain_copy(u, z, True).wait_recv()
            fsum[u, z] += upf[u, z]

        @pl.when(z < nz - 1)
        def _():
            fin_chain_copy(u, z, False).wait_recv()
            fsum[u, z] += dnf[u, z]

        for i in range(su):
            for part in range(2):
                out_ref[last, part, u * su + i] = fsum[u, z, i, part]

    flush(bands_sent)
    flush(sends)


def per_device(history, self_energy, green_row, propagator):
    n_tgt, n_hist = lax.axis_size("tgt"), lax.axis_size("hist")
    _, sh, tt, n, _ = history.shape
    hp, band, last = n_hist // n_tgt, n // n_hist, STEPS - 1
    nz = n_hist // hp
    norm = float(sh * n_hist * n) ** (-0.5)
    n_cut = hp * CUTS
    su = tt // n_cut
    vmem, sem = pltpu.VMEM, pltpu.SemaphoreType.DMA
    return pl.pallas_call(
        functools.partial(kernel, n_tgt, n_hist, norm),
        out_shape=jax.ShapeDtypeStruct((STEPS, 2, tt, band, n), F32),
        in_specs=[pl.BlockSpec(memory_space=pl.ANY)] * 4,
        out_specs=pl.BlockSpec(memory_space=pltpu.VMEM),
        scratch_shapes=[
            vmem((tt, 2, sh, n, n), F32),
            vmem((tt, 3 * sh * n, 2 * n), BF16),
            vmem((2 * n, 3 * sh * n), BF16),
            vmem((tt, 2 * n, 2 * n), F32),
            vmem((STEPS, 2, sh, n, n), F32),
            vmem((2, tt, n, n), F32),
            vmem((2, n, n), F32),
            vmem((last, hp, sh, 2, n, n), F32),
            vmem((last, hp, sh, 2, n, n), F32),
            vmem((last, sh, 2, n, n), F32),
            vmem((last, sh, 2, n, n), F32),
            vmem((last, sh, 2, n, n), F32),
            vmem((last, 2, sh, n, n), F32),
            vmem((STEPS, sh, 3 * n, 2 * n), BF16),
            vmem((sh, 2, n, n), F32),
            vmem((STEPS, STEPS, 2, n, n), F32),
            vmem((STEPS, 2 * n, 3 * n), BF16),
            vmem((last, 2, tt, band, n), F32),
            vmem((n_cut, nz, hp, su, 2, band, n), F32),
            vmem((n_cut, hp, nz, su, 2, band, n), F32),
            vmem((n_cut, nz, su, 2, band, n), F32),
            vmem((n_cut, nz, su, 2, band, n), F32),
            vmem((n_cut, nz, su, 2, band, n), F32),
            sem((tt,)),
            sem((3,)),
            sem((last, hp, sh)),
            sem((last, hp, sh)),
            sem((last, sh, PIECES)),
            sem((last, sh, PIECES)),
            sem((last, sh, PIECES)),
            sem((STEPS, 2, PIECES, sh)),
            sem((STEPS, PIECES, sh)),
            sem((STEPS, STEPS)),
            sem((STEPS, STEPS, hp)),
            sem((STEPS, STEPS)),
            sem((last, n_hist)),
            sem((last, hp)),
            sem((n_cut, hp)),
            sem((n_cut, hp)),
            sem((n_cut, nz)),
            sem((n_cut, nz)),
            sem((n_cut, nz)),
        ],
        compiler_params=pltpu.CompilerParams(
            collective_id=0, has_side_effects=True, vmem_limit_bytes=56 * 2**20
        ),
    )(history, self_energy, green_row, propagator)


def solution(mesh):
    in_specs = (
        P(None, "hist", "tgt", None, None),
        P(None, "hist", None, None),
        P(None, "tgt", None, None),
        P(),
    )
    out_specs = P(None, None, "tgt", "hist", None)
    return jax.shard_map(
        per_device, mesh=mesh, in_specs=in_specs, out_specs=out_specs, check_vma=False
    )
```
